512 devices in a mesh: src: 32 (over z, y_hi), tgt: 16 (over x, y_lo, core).
Axes of the slice: x: 4, y: 4 (y_hi: 2, y_lo: 2; y = y_hi * 2 + y_lo), z: 16, core: 2. Of those that a mesh axis runs over, the one named last changes fastest.
Arguments:
- edge_state: bfloat16 [32, 16, 512, 1024], P('src', 'tgt'), may hold values from -8 to 8
- atom_state: bfloat16 [32, 256, 256], P('src', 'tgt'), may hold values from -6 to 6
- edge_source: int32 [32, 16, 512], P('src', 'tgt'), may hold values from 0 to 255, as said below
- trip_source: int32 [32, 16, 4096], P('src', 'tgt'), may hold values from 0 to 16383
- trip_target: int32 [32, 16, 4096], P('src', 'tgt'), may hold values from 0 to 511
- trip_count: int32 [32, 16], P('src', 'tgt'), may hold values from 1024 to 4096, as said below
- trip_basis: bfloat16 [32, 16, 16, 4096], P('src', 'tgt'), may hold values from -6 to 6
- reverse_perm: int32 [32, 16, 512], P('src', 'tgt'), may hold values from 0 to 511, each once within a row
- down_proj: bfloat16 [1024, 64], replicated, may hold values from -0.1875 to 0.1875
- bilinear: bfloat16 [1024, 64], replicated, may hold values from -0.1875 to 0.1875
- up_forward: bfloat16 [64, 1024], replicated, may hold values from -0.75 to 0.75
- up_reverse: bfloat16 [64, 1024], replicated, may hold values from -0.75 to 0.75
- res_first: bfloat16 [1024, 1024], P('tgt'), may hold values from -0.1875 to 0.1875
- res_second: bfloat16 [1024, 1024], P('tgt'), may hold values from -0.1875 to 0.1875
- atom_proj: bfloat16 [1024, 256], replicated, may hold values from -0.1875 to 0.1875
- atom_self: bfloat16 [256, 256], replicated, may hold values from -0.375 to 0.375
- atom_back: bfloat16 [256, 1024], replicated, may hold values from -0.375 to 0.375
Outputs:
- edge_new: bfloat16 [32, 16, 512, 1024], P('src', 'tgt')
- atom_new: bfloat16 [32, 256, 256], P('src', 'tgt')
The draws below stay inside these ranges and needn't reach their ends.
Inputs may be any that keep to these rules, and one draw needn't show every extreme that they name: `trip_count`: each tile has 1024 to 4096 live triplet slots, the first ones; some tile has all 4096 live in every draw. `edge_source`: edge slot e of a tile has its source atom in share e mod 16 of the block, that is among atoms of that share times 16 to the next multiple of 16.
All inputs are finite; a program needn't handle non-finite values.
Results may differ from the reference program's by a relative error of at most 0.012.
Values may be sent and summed in bfloat16 or wider, within the bound.
No kernel may reach another device: no remote copies, remote signals or barrier semaphores. Data moves between devices by JAX's collectives and lax.ppermute only.
A program may use at most 64 MiB of HBM per device.

```python
import math
import jax
import jax.numpy as jnp
from jax import lax

DE = 1024
DT = 64
DA = 256
NBASIS = 16
E_DEV = 512
TRIP_DEV = 4096
ATOM_DEV = 16
A_BLK = 256
N_SRC = 32
N_TGT = 16


def draw_edge_state(key, part):
    key = jax.random.fold_in(key, 5)
    first_key = jax.random.fold_in(key, 0)
    column_pos = jnp.arange(N_TGT, dtype=jnp.float32) / max(N_TGT - 1, 1)
    values = jnp.clip(jax.random.normal(first_key, (N_SRC, N_TGT, E_DEV, DE), jnp.float32), -4.0, 4.0)
    column_scale = 0.6 + 1.2 * column_pos
    values = values * column_scale[None, :, None, None]
    return values.astype(jnp.bfloat16)


def draw_trip_count(key, part):
    key = jax.random.fold_in(key, 7)
    first_key, second_key = jax.random.split(key)
    counts = jax.random.randint(first_key, (N_SRC * N_TGT,), TRIP_DEV // 4, TRIP_DEV + 1)
    chosen = jax.random.randint(second_key, (), 0, N_SRC * N_TGT)
    counts = jnp.where(jnp.arange(N_SRC * N_TGT) == chosen, TRIP_DEV, counts)
    return counts.reshape(N_SRC, N_TGT).astype(jnp.int32)


def draw_edge_source(key, part):
    key = jax.random.fold_in(key, 11)
    piece_rows = E_DEV // (N_SRC * N_TGT)
    slots = jnp.arange(E_DEV, dtype=jnp.int32)
    shares = slots // piece_rows % N_TGT
    offsets = jax.random.randint(key, (N_SRC, N_TGT, E_DEV), 0, ATOM_DEV)
    values = (shares[None, None, :] * ATOM_DEV + offsets).reshape(-1)
    places = jnp.arange(values.shape[0], dtype=jnp.int32)
    values = jnp.where(places == 0, 0, values)
    values = jnp.where(places == values.shape[0] - 1, A_BLK - 1, values)
    return values.reshape(N_SRC, N_TGT, E_DEV).astype(jnp.int32)


def with_ends(values, key, smallest, high):
    longest = values.shape.index(max(values.shape))
    spots = []
    for shift in (0, 1):
        where = [jax.random.randint(jax.random.fold_in(key, axis), (), 0, length) for axis, length in enumerate(values.shape)]
        where[longest] = (where[longest] + shift) % values.shape[longest]
        spots.append(tuple(where))
    return values.at[spots[0]].set(smallest).at[spots[1]].set(high)


def levels(own_key, extent, shards, least, high):
    loudness = 1.0
    for axis_at, blocks in shards:
        steps = jax.random.uniform(jax.random.fold_in(jax.random.fold_in(own_key, 6), axis_at), (blocks,), jnp.float32, least / len(shards), high / len(shards))
        loudness = loudness * jnp.repeat(jnp.exp(steps), extent[axis_at] // blocks).reshape((-1,) + (1,) * (len(extent) - 1 - axis_at))
    return loudness


def normal_values(stream_key, dims, deviation, limit, cuts=(), held_as=jnp.bfloat16):
    array = jax.random.normal(stream_key, dims, jnp.float32) * deviation
    if len(cuts) > 0:
        array = levels(stream_key, dims, cuts, -0.22, 0.18) * array
    return jnp.clip(array, min=-limit, max=limit).astype(held_as)


def setup_inputs(seed: int = 0) -> dict:
    streams_of = jax.random.split(jax.random.key(seed), 18)
    edge_state = draw_edge_state(jax.random.fold_in(streams_of[17], 71), 0)
    atom_state = normal_values(streams_of[1], (N_SRC, A_BLK, DA), 1.0, 6.0, ((0, 32), (1, 16)))
    edge_source = draw_edge_source(jax.random.fold_in(streams_of[17], 71), 0)
    trip_source = with_ends(jax.random.randint(streams_of[3], (N_SRC, N_TGT, TRIP_DEV), 0, N_SRC * E_DEV), jax.random.fold_in(streams_of[3], 1), 0, (N_SRC * E_DEV) - 1).astype(jnp.int32)
    trip_target = with_ends(jax.random.randint(streams_of[4], (N_SRC, N_TGT, TRIP_DEV), 0, E_DEV), jax.random.fold_in(streams_of[4], 1), 0, E_DEV - 1).astype(jnp.int32)
    trip_count = draw_trip_count(jax.random.fold_in(streams_of[17], 71), 0)
    trip_basis = normal_values(streams_of[6], (N_SRC, N_TGT, NBASIS, TRIP_DEV), 1.0, 6.0, ((0, 32), (1, 16)))
    reverse_perm = jax.vmap(lambda own: jax.random.permutation(own, E_DEV))(jax.random.split(streams_of[7], N_SRC * N_TGT)).reshape((N_SRC, N_TGT, E_DEV)).astype(jnp.int32)
    down_proj = normal_values(streams_of[8], (DE, DT), DE ** -0.5, 0.1875)
    bilinear = normal_values(streams_of[9], (NBASIS * DT, DT), (NBASIS * DT) ** -0.5, 0.1875)
    up_forward = normal_values(streams_of[10], (DT, DE), DT ** -0.5, 0.75)
    up_reverse = normal_values(streams_of[11], (DT, DE), DT ** -0.5, 0.75)
    res_first = normal_values(streams_of[12], (DE, DE), DE ** -0.5, 0.1875, ((0, 16),))
    res_second = normal_values(streams_of[13], (DE, DE), DE ** -0.5, 0.1875, ((0, 16),))
    atom_proj = normal_values(streams_of[14], (DE, DA), DE ** -0.5, 0.1875)
    atom_self = normal_values(streams_of[15], (DA, DA), DA ** -0.5, 0.375)
    atom_back = normal_values(streams_of[16], (DA, DE), DA ** -0.5, 0.375)
    return {"edge_state": edge_state, "atom_state": atom_state, "edge_source": edge_source, "trip_source": trip_source, "trip_target": trip_target, "trip_count": trip_count, "trip_basis": trip_basis, "reverse_perm": reverse_perm, "down_proj": down_proj, "bilinear": bilinear, "up_forward": up_forward, "up_reverse": up_reverse, "res_first": res_first, "res_second": res_second, "atom_proj": atom_proj, "atom_self": atom_self, "atom_back": atom_back}


INV_THREE = 1.0 / math.sqrt(3.0)
INV_TWO = 1.0 / math.sqrt(2.0)

def project(values, weight):
    flat = values.reshape(-1, values.shape[-1])
    result = jnp.dot(flat, weight, preferred_element_type=jnp.float32)
    return result.reshape(values.shape[:-1] + (weight.shape[1],))

def reference(edge_state, atom_state, edge_source, trip_source, trip_target, trip_count, trip_basis, reverse_perm, down_proj, bilinear, up_forward, up_reverse, res_first, res_second, atom_proj, atom_self, atom_back):
    down_msg = jax.nn.silu(project(edge_state, down_proj)).astype(jnp.bfloat16)
    tile_total = N_SRC * N_TGT

    def contract(pieces):
        target_col, source_idx, target_idx, live_count, basis_tile = pieces
        column = jnp.take(down_msg, target_col, axis=1).reshape(N_SRC * E_DEV, DT)
        picked = jnp.take(column, source_idx, axis=0).astype(jnp.float32)
        outer_prod = (basis_tile.T.astype(jnp.float32)[:, :, None] * picked[:, None, :]).reshape(TRIP_DEV, NBASIS * DT)
        outer_prod = lax.optimization_barrier(outer_prod.astype(jnp.bfloat16)).astype(jnp.float32)
        valid_mask = (jnp.arange(TRIP_DEV, dtype=jnp.int32) < live_count).astype(jnp.float32)
        summed = jax.ops.segment_sum(outer_prod * valid_mask[:, None], target_idx, num_segments=E_DEV)
        return jnp.dot(summed.astype(jnp.bfloat16), bilinear, preferred_element_type=jnp.float32).astype(jnp.bfloat16)
    target_cols = (jnp.arange(tile_total, dtype=jnp.int32) % N_TGT).astype(jnp.int32)
    trip_msg = lax.map(contract, (target_cols, trip_source.reshape(tile_total, TRIP_DEV), trip_target.reshape(tile_total, TRIP_DEV), trip_count.reshape(tile_total), trip_basis.reshape(tile_total, NBASIS, TRIP_DEV)))
    trip_msg = trip_msg.reshape(N_SRC, N_TGT, E_DEV, DT)
    forward_out = jax.nn.silu(project(trip_msg, up_forward)).astype(jnp.bfloat16)
    reverse_out = jax.nn.silu(project(trip_msg, up_reverse)).astype(jnp.bfloat16)
    piece_rows = E_DEV // (N_SRC * N_TGT)
    arranged = reverse_out.reshape(N_SRC, N_TGT, N_SRC, N_TGT, piece_rows, DE).transpose(2, 3, 0, 1, 4, 5).reshape(N_SRC, N_TGT, E_DEV, DE)
    mirrored = jnp.take_along_axis(arranged, reverse_perm[..., None], axis=2)
    mixed_state = ((edge_state.astype(jnp.float32) + forward_out.astype(jnp.float32) + mirrored.astype(jnp.float32)) * INV_THREE).astype(jnp.bfloat16)
    inner_act = jax.nn.silu(project(mixed_state, res_first)).astype(jnp.bfloat16)
    skipped = ((mixed_state.astype(jnp.float32) + jax.nn.silu(project(inner_act, res_second))) * INV_TWO).astype(jnp.bfloat16)
    atom_terms = jax.nn.silu(project(skipped, atom_proj)).astype(jnp.bfloat16)

    def block_sum(terms, sources):
        return jax.ops.segment_sum(terms.reshape(-1, DA).astype(jnp.float32), sources.reshape(-1), num_segments=ATOM_DEV * N_TGT)
    atom_sums = jax.vmap(block_sum)(atom_terms, edge_source).astype(jnp.bfloat16)
    atom_new = (atom_state.astype(jnp.float32) + jax.nn.silu(project(atom_sums, atom_self))).astype(jnp.bfloat16)

    def pick_block(atom_block, sources):
        return jnp.take(atom_block, sources.reshape(-1), axis=0)
    source_feats = jax.vmap(pick_block)(atom_new, edge_source).reshape(N_SRC, N_TGT, E_DEV, DA)
    edge_new = (skipped.astype(jnp.float32) + jax.nn.silu(project(source_feats, atom_back))).astype(jnp.bfloat16)
    return (edge_new, atom_new)
```

```python
import math

import jax
import jax.numpy as jnp
from jax import lax
from jax.experimental import pallas as pl
from jax.experimental.pallas import tpu as pltpu
from jax.sharding import PartitionSpec as P

INV_THREE = 1.0 / math.sqrt(3.0)
INV_TWO = 1.0 / math.sqrt(2.0)
F32 = jnp.float32
BF16 = jnp.bfloat16

Z, YH, NT = 16, 2, 16
NS = Z * YH
FAR = 8
BLOCK = 512


def silu(v):
    return v * (0.5 * jnp.tanh(0.5 * v) + 0.5)


def dot(a, b, ca=1, cb=0):
    return lax.dot_general(a, b, (((ca,), (cb,)), ((), ())), preferred_element_type=F32)


def params(mb=48):
    return pltpu.CompilerParams(vmem_limit_bytes=mb * 1024 * 1024)


VM = pl.BlockSpec(memory_space=pltpu.VMEM)
SM = pl.BlockSpec(memory_space=pltpu.SMEM)
HB = pl.BlockSpec(memory_space=pl.ANY)


def down_kernel(x_ref, w_ref, o_ref):
    y = silu(dot(x_ref[...], w_ref[...], 1, 1)).astype(BF16)
    half = y.shape[0] // 2
    packed = jnp.concatenate([y[:half], y[half:]], axis=1)
    for i in range(o_ref.shape[0]):
        o_ref[i] = packed


def contract_kernel(
    pos_ref, cnt_ref, tgt_ref, basis_ref, bil_ref, b0, b1, b2, b3, tm_ref, send_ref, col, picked, acc
):
    trips = tgt_ref.shape[1]
    edges, width = tm_ref.shape
    lanes = 2 * width
    low = lax.broadcasted_iota(jnp.int32, (256, lanes), 1) < width

    def widen(i, c):
        for n, ref in enumerate((b0, b1, b2, b3)):
            v = ref[i].astype(F32)
            w = pltpu.roll(v, width, 1)
            at = (n * FAR + i) * 512
            col[pl.ds(pl.multiple_of(at, 512), 256), :] = jnp.where(low, v, w)
            col[pl.ds(pl.multiple_of(at + 256, 256), 256), :] = jnp.where(low, w, v)
        return c

    lax.fori_loop(0, FAR, widen, 0)

    unroll = 32

    def fetch(i, c):
        base = pl.multiple_of(i * unroll, unroll)
        for j in range(unroll):
            picked[pl.ds(base + j, 1), :] = col[pl.ds(pos_ref[0, base + j], 1), :]
        return c

    lax.fori_loop(0, trips // unroll, fetch, 0)

    count = cnt_ref[0, 0]
    nb = basis_ref.shape[0]
    full = nb * width
    expand = (
        lax.broadcasted_iota(jnp.int32, (nb, full), 1) // width
        == lax.broadcasted_iota(jnp.int32, (nb, full), 0)
    ).astype(BF16)
    edge_ids = lax.broadcasted_iota(jnp.int32, (edges, BLOCK), 0)
    slot_ids = lax.broadcasted_iota(jnp.int32, (1, BLOCK), 1)
    acc[...] = jnp.zeros_like(acc)

    def block(i, c):
        at = pl.multiple_of(i * BLOCK, BLOCK)
        spread = dot(basis_ref[:, pl.ds(at, BLOCK)], expand, 0, 0).astype(BF16)
        rows = picked[pl.ds(at, BLOCK), :].astype(BF16)
        outer = spread * jnp.concatenate([rows] * (nb // 2), axis=1)
        msg = dot(outer, bil_ref[...], 1, 1)
        hi = msg.astype(BF16)
        lo = (msg - hi.astype(F32)).astype(BF16)
        tgt = jnp.where(slot_ids + at < count, tgt_ref[:, pl.ds(at, BLOCK)], -1)
        hot = jnp.where(edge_ids == tgt, 1.0, 0.0).astype(BF16)
        acc[...] += dot(hot, jnp.concatenate([hi, lo], axis=1))
        return c

    lax.fori_loop(0, trips // BLOCK, block, 0)
    total = acc[...]
    msg = (total[:, :width] + total[:, width:]).astype(BF16)
    tm_ref[...] = msg
    acc[:, :width] = msg.astype(F32)
    for t in range(NT):
        first = acc[pl.ds(t, NT, stride=NT), :]
        second = acc[pl.ds(NT * NT + t, NT, stride=NT), :]
        send_ref[t] = jnp.concatenate([first[:, :width], second[:, :width]], axis=1).astype(BF16)


def turn_kernel(x_ref, o_ref, tmp):
    width = x_ref.shape[2] // 2
    tmp[...] = x_ref[...].reshape(tmp.shape).astype(F32)
    for s in range(NT):
        first = tmp[pl.ds(s, 8, stride=NT), :]
        second = tmp[pl.ds(8 * NT + s, 8, stride=NT), :]
        o_ref[s] = jnp.concatenate([first[:, :width], second[:, :width]], axis=1).astype(BF16)
        o_ref[NT + s] = jnp.concatenate([first[:, width:], second[:, width:]], axis=1).astype(BF16)


def edge_kernel(
    x_ref, tm_ref, got_ref, perm_ref, src_ref, upf_ref, upr_ref, w1_ref, w2_ref, proj_ref,
    skip_ref, part_ref, w1, w2, sems,
):
    load1 = pltpu.make_async_copy(w1_ref, w1, sems.at[0])
    load2 = pltpu.make_async_copy(w2_ref, w2, sems.at[1])
    load1.start()
    load2.start()
    edges = x_ref.shape[0]
    width = tm_ref.shape[1]
    got = got_ref[...]
    got = jnp.concatenate([got[:, :width], got[:, width:]], axis=0)
    perm = perm_ref[...]
    row = ((perm >> 3) & 1) * (edges // 2) + (perm >> 4) * 8 + (perm & 7)
    hot = jnp.where(
        lax.broadcasted_iota(jnp.int32, (edges, edges), 0) == row, 1.0, 0.0
    ).astype(BF16)
    mirror_msg = dot(hot, got, 0, 0).astype(BF16)
    forward_out = silu(dot(tm_ref[...], upf_ref[...])).astype(BF16)
    mirrored = silu(dot(mirror_msg, upr_ref[...])).astype(BF16)
    mixed = (
        (x_ref[...].astype(F32) + forward_out.astype(F32) + mirrored.astype(F32)) * INV_THREE
    ).astype(BF16)
    load1.wait()
    inner = silu(dot(mixed, w1[...])).astype(BF16)
    load2.wait()
    skipped = ((mixed.astype(F32) + silu(dot(inner, w2[...]))) * INV_TWO).astype(BF16)
    skip_ref[...] = skipped
    terms = silu(dot(skipped, proj_ref[...])).astype(BF16)
    atoms = part_ref.shape[0]
    own = jnp.where(
        lax.broadcasted_iota(jnp.int32, (atoms, edges), 0) == src_ref[...], 1.0, 0.0
    ).astype(BF16)
    part_ref[...] = dot(own, terms).astype(BF16)


def atom_kernel(parts_ref, state_ref, w_ref, new_ref, send_ref):
    total = parts_ref[0].astype(F32)
    for i in range(1, NT):
        total = total + parts_ref[i].astype(F32)
    new = (state_ref[...].astype(F32) + silu(dot(total.astype(BF16), w_ref[...]))).astype(BF16)
    new_ref[...] = new
    for i in range(NT):
        send_ref[i] = new


def final_kernel(skip_ref, block_ref, src_ref, back_ref, o_ref):
    atoms = block_ref.shape[0]
    edges = skip_ref.shape[0]
    own = jnp.where(
        lax.broadcasted_iota(jnp.int32, (atoms, edges), 0) == src_ref[...], 1.0, 0.0
    ).astype(BF16)
    feats = dot(own, block_ref[...], 0, 0).astype(BF16)
    o_ref[...] = (skip_ref[...].astype(F32) + silu(dot(feats, back_ref[...]))).astype(BF16)


def shift(d):
    return [(z * YH + h, ((z + d) % Z) * YH + h) for z in range(Z) for h in range(YH)]


def shift_two():
    return [
        (z * YH + h, ((z + (2 if z % 2 == 0 else -2)) % Z) * YH + h)
        for z in range(Z)
        for h in range(YH)
    ]


def struct(shape, dtype=BF16):
    return jax.ShapeDtypeStruct(shape, dtype)


def local(
    edge_state,
    atom_state,
    edge_source,
    trip_source,
    trip_target,
    trip_count,
    trip_basis,
    reverse_perm,
    down_proj,
    bilinear,
    up_forward,
    up_reverse,
    res_first,
    res_second,
    atom_proj,
    atom_self,
    atom_back,
):
    rows = edge_state[0, 0]
    edges, wide = rows.shape
    width = down_proj.shape[1]
    trips = trip_source.shape[2]

    far = pl.pallas_call(
        down_kernel,
        out_shape=struct((FAR, edges // 2, 2 * width)),
        in_specs=[VM] * 2,
        out_specs=VM,
        compiler_params=params(),
    )(rows, down_proj.T)

    groups = [
        [((z0 + 4 * i) % Z) * YH + h for i in range(4) for h in range(YH)] for z0 in range(4)
    ]
    near = lax.all_to_all(
        far, "src", split_axis=0, concat_axis=0, tiled=True, axis_index_groups=groups
    )
    from_next = lax.ppermute(near, "src", shift(-1))
    from_prev = lax.ppermute(near, "src", shift(1))
    from_two = lax.ppermute(near, "src", shift_two())

    first_all = lax.all_gather(res_first, "tgt", axis=0, tiled=True)
    second_all = lax.all_gather(res_second, "tgt", axis=0, tiled=True)

    my_z = lax.axis_index("src") // YH
    ids = trip_source[0]
    q = ids >> 9
    zq = q >> 1
    pos = (((zq - my_z) & 3) * FAR + (zq >> 2) * 2 + (q & 1)) * edges + (ids & (edges - 1))

    tm, send = pl.pallas_call(
        contract_kernel,
        out_shape=(struct((edges, width)), struct((NT, NT, 2 * width))),
        in_specs=[SM, SM] + [VM] * 7,
        out_specs=(VM, VM),
        scratch_shapes=[
            pltpu.VMEM((NS * edges, 2 * width), F32),
            pltpu.VMEM((trips, 2 * width), F32),
            pltpu.VMEM((edges, 2 * width), F32),
        ],
        compiler_params=params(),
    )(
        pos,
        trip_count,
        trip_target[0],
        trip_basis[0, 0],
        bilinear.T,
        near,
        from_next,
        from_two,
        from_prev,
    )

    got = lax.all_to_all(send, "tgt", split_axis=0, concat_axis=0, tiled=True)
    turned = pl.pallas_call(
        turn_kernel,
        out_shape=struct((NS, 8, 2 * width)),
        in_specs=[VM],
        out_specs=VM,
        scratch_shapes=[pltpu.VMEM((NT * NT, 2 * width), F32)],
        compiler_params=params(),
    )(got)
    arrived = lax.all_to_all(turned, "src", split_axis=0, concat_axis=0, tiled=True)

    atoms = atom_state.shape[1] * NT
    da = atom_state.shape[2]
    skipped, part = pl.pallas_call(
        edge_kernel,
        out_shape=(struct((edges, wide)), struct((atoms, da))),
        in_specs=[VM] * 7 + [HB] * 2 + [VM],
        out_specs=(VM, VM),
        scratch_shapes=[
            pltpu.VMEM((wide, wide), BF16),
            pltpu.VMEM((wide, wide), BF16),
            pltpu.SemaphoreType.DMA((2,)),
        ],
        compiler_params=params(),
    )(
        rows,
        tm,
        arrived.reshape(edges // 2, 2 * width),
        reverse_perm[0],
        edge_source[0],
        up_forward,
        up_reverse,
        first_all,
        second_all,
        atom_proj,
    )

    parts = lax.all_to_all(
        part.reshape(NT, atoms // NT, da), "tgt", split_axis=0, concat_axis=0, tiled=True
    )
    atom_new, spread = pl.pallas_call(
        atom_kernel,
        out_shape=(struct((atoms // NT, da)), struct((NT, atoms // NT, da))),
        in_specs=[VM] * 3,
        out_specs=(VM, VM),
        compiler_params=params(),
    )(parts, atom_state[0], atom_self)
    block = lax.all_to_all(spread, "tgt", split_axis=0, concat_axis=0, tiled=True)
    edge_new = pl.pallas_call(
        final_kernel,
        out_shape=struct((edges, wide)),
        in_specs=[VM] * 4,
        out_specs=VM,
        compiler_params=params(),
    )(skipped, block.reshape(atoms, da), edge_source[0], atom_back)
    return (edge_new[None, None], atom_new[None])


def solution(mesh):
    return jax.shard_map(
        local,
        mesh=mesh,
        in_specs=(
            P("src", "tgt", None, None),
            P("src", "tgt", None),
            P("src", "tgt", None),
            P("src", "tgt", None),
            P("src", "tgt", None),
            P("src", "tgt"),
            P("src", "tgt", None, None),
            P("src", "tgt", None),
            P(),
            P(),
            P(),
            P(),
            P("tgt", None),
            P("tgt", None),
            P(),
            P(),
            P(),
        ),
        out_specs=(P("src", "tgt", None, None), P("src", "tgt", None)),
        check_vma=False,
    )
```

```python
import math

import jax
import jax.numpy as jnp
from jax import lax
from jax.experimental import pallas as pl
from jax.experimental.pallas import tpu as pltpu
from jax.sharding import PartitionSpec as P

INV_THREE = 1.0 / math.sqrt(3.0)
INV_TWO = 1.0 / math.sqrt(2.0)
F32 = jnp.float32
BF16 = jnp.bfloat16

Z, YH, NT = 16, 2, 16
NS = Z * YH
FAR = 8
XS = 4
PEER = (0, 2, 1, 3)
BLOCK = 1024


def silu(v):
    return v * (0.5 * jnp.tanh(0.5 * v) + 0.5)


def dot(a, b, ca=1, cb=0):
    return lax.dot_general(a, b, (((ca,), (cb,)), ((), ())), preferred_element_type=F32)


def params(mb=48):
    return pltpu.CompilerParams(vmem_limit_bytes=mb * 1024 * 1024)


VM = pl.BlockSpec(memory_space=pltpu.VMEM)
SM = pl.BlockSpec(memory_space=pltpu.SMEM)
HB = pl.BlockSpec(memory_space=pl.ANY)


def down_kernel(x_ref, w_ref, a_ref, b_ref, o_ref, ab_ref):
    ab_ref[0] = a_ref[...]
    ab_ref[1] = b_ref[...]
    y = silu(dot(x_ref[...], w_ref[...], 1, 1)).astype(BF16)
    half = y.shape[0] // 2
    packed = jnp.concatenate([y[:half], y[half:]], axis=1)
    for i in range(o_ref.shape[0]):
        o_ref[i] = packed


def contract_kernel(
    pos_ref, cnt_ref, ids_ref, tgt_ref, basis_ref, bil_ref, b0, b1, b2, b3,
    tm_ref, send_ref, col, rows_a, rows_b, acc, total,
):
    trips = tgt_ref.shape[1]
    edges, width = tm_ref.shape
    lanes = 2 * width
    step = rows_a.shape[0]

    def widen(i, c):
        for n, ref in enumerate((b0, b1, b2, b3)):
            at = pl.multiple_of((n * FAR + i) * 256, 256)
            col[pl.ds(at, 256), :] = ref[i].astype(F32)
        return c

    lax.fori_loop(0, FAR, widen, 0)

    count = cnt_ref[0, 0]
    nb = basis_ref.shape[0]
    eye = (
        lax.broadcasted_iota(jnp.int32, (lanes, lanes), 0)
        == lax.broadcasted_iota(jnp.int32, (lanes, lanes), 1)
    ).astype(BF16)
    edge_ids = lax.broadcasted_iota(jnp.int32, (edges, step), 0)
    slot_ids = lax.broadcasted_iota(jnp.int32, (1, step), 1)
    total[...] = jnp.zeros_like(total)

    def fetch(dst, at):
        for j in range(step):
            dst[j : j + 1, :] = col[pl.ds(pos_ref[0, at + j], 1), :]

    def block(at, rows):
        both = dot(eye, rows[...].astype(BF16), 1, 1)
        upper = ((ids_ref[:, at : at + step] >> 8) & 1) == 1
        msg = jnp.where(upper, both[width:], both[:width]).astype(BF16)
        basis = basis_ref[:, at : at + step]
        outer = jnp.concatenate([basis[c : c + 1, :] * msg for c in range(nb)], axis=0)
        out = dot(bil_ref[...], outer)
        hi = out.astype(BF16)
        lo = (out - hi.astype(F32)).astype(BF16)
        tgt = jnp.where(slot_ids + at < count, tgt_ref[:, at : at + step], -1)
        hot = jnp.where(edge_ids == tgt, 1.0, 0.0).astype(BF16)
        total[...] += dot(jnp.concatenate([hi, lo], axis=0), hot, 1, 1)

    held = (rows_a, rows_b)
    fetch(held[0], 0)
    for i in range(trips // step):
        if (i + 1) * step < trips:
            fetch(held[(i + 1) % 2], (i + 1) * step)
        block(i * step, held[i % 2])
    msg = jnp.transpose(total[:width, :] + total[width:, :]).astype(BF16)
    tm_ref[...] = msg
    acc[:, :width] = msg.astype(F32)
    for t in range(NT):
        first = acc[pl.ds(t, NT, stride=NT), :]
        second = acc[pl.ds(NT * NT + t, NT, stride=NT), :]
        send_ref[t] = jnp.concatenate([first[:, :width], second[:, :width]], axis=1).astype(BF16)


def turn_kernel(x_ref, o_ref, tmp):
    width = x_ref.shape[2] // 2
    tmp[...] = x_ref[...].reshape(tmp.shape).astype(F32)
    for s in range(NT):
        first = tmp[pl.ds(s, 8, stride=NT), :]
        second = tmp[pl.ds(8 * NT + s, 8, stride=NT), :]
        o_ref[s] = jnp.concatenate([first[:, :width], second[:, :width]], axis=1).astype(BF16)
        o_ref[NT + s] = jnp.concatenate([first[:, width:], second[:, width:]], axis=1).astype(BF16)


def edge_kernel(
    me_ref, x_ref, tm_ref, got_ref, perm_ref, src_ref, upf_ref, upr_ref, proj_ref,
    wa_ref, wb_ref, wc_ref, wd_ref, skip_ref, part_ref, w1, w2, sems,
):
    me = me_ref[0, 0]
    loads = ([], [])
    for k, w in enumerate((w1, w2)):
        for i, ref in enumerate((wa_ref, wb_ref, wc_ref, wd_ref)):
            for j in range(XS):
                at = (((((me >> 2) + j) & 3) * 4 + ((me & 3) ^ PEER[i]))) * ref.shape[2]
                at = pl.multiple_of(at, 64)
                loads[k].append(
                    pltpu.make_async_copy(
                        ref.at[j, k], w.at[pl.ds(at, ref.shape[2]), :], sems.at[k, i * XS + j]
                    )
                )
    for load in loads[0] + loads[1]:
        load.start()
    edges = x_ref.shape[0]
    width = tm_ref.shape[1]
    got = got_ref[...]
    got = jnp.concatenate([got[:, :width], got[:, width:]], axis=0)
    perm = perm_ref[...]
    row = ((perm >> 3) & 1) * (edges // 2) + (perm >> 4) * 8 + (perm & 7)
    hot = jnp.where(
        lax.broadcasted_iota(jnp.int32, (edges, edges), 0) == row, 1.0, 0.0
    ).astype(BF16)
    mirror_msg = dot(hot, got, 0, 0).astype(BF16)
    forward_out = silu(dot(tm_ref[...], upf_ref[...])).astype(BF16)
    mirrored = silu(dot(mirror_msg, upr_ref[...])).astype(BF16)
    mixed = (
        (x_ref[...].astype(F32) + forward_out.astype(F32) + mirrored.astype(F32)) * INV_THREE
    ).astype(BF16)
    for load in loads[0]:
        load.wait()
    inner = silu(dot(mixed, w1[...])).astype(BF16)
    for load in loads[1]:
        load.wait()
    skipped = ((mixed.astype(F32) + silu(dot(inner, w2[...]))) * INV_TWO).astype(BF16)
    skip_ref[...] = skipped
    terms = silu(dot(skipped, proj_ref[...])).astype(BF16)
    atoms = part_ref.shape[0]
    own = jnp.where(
        lax.broadcasted_iota(jnp.int32, (atoms, edges), 0) == src_ref[...], 1.0, 0.0
    ).astype(BF16)
    part_ref[...] = dot(own, terms).astype(BF16)


def atom_kernel(parts_ref, state_ref, w_ref, new_ref, send_ref):
    total = parts_ref[0].astype(F32)
    for i in range(1, NT):
        total = total + parts_ref[i].astype(F32)
    new = (state_ref[...].astype(F32) + silu(dot(total.astype(BF16), w_ref[...]))).astype(BF16)
    new_ref[...] = new
    for i in range(NT):
        send_ref[i] = new


def final_kernel(skip_ref, block_ref, src_ref, back_ref, o_ref):
    atoms = block_ref.shape[0]
    edges = skip_ref.shape[0]
    own = jnp.where(
        lax.broadcasted_iota(jnp.int32, (atoms, edges), 0) == src_ref[...], 1.0, 0.0
    ).astype(BF16)
    feats = dot(own, block_ref[...], 0, 0).astype(BF16)
    o_ref[...] = (skip_ref[...].astype(F32) + silu(dot(feats, back_ref[...]))).astype(BF16)


def shift(d):
    return [(z * YH + h, ((z + d) % Z) * YH + h) for z in range(Z) for h in range(YH)]


def shift_two():
    return [
        (z * YH + h, ((z + (2 if z % 2 == 0 else -2)) % Z) * YH + h)
        for z in range(Z)
        for h in range(YH)
    ]


def along_x(d):
    return [(t, ((t // 4 + d) % XS) * 4 + t % 4) for t in range(NT)]


def across(bit):
    return [(t, t ^ bit) for t in range(NT)]


def struct(shape, dtype=BF16):
    return jax.ShapeDtypeStruct(shape, dtype)


def local(
    edge_state,
    atom_state,
    edge_source,
    trip_source,
    trip_target,
    trip_count,
    trip_basis,
    reverse_perm,
    down_proj,
    bilinear,
    up_forward,
    up_reverse,
    res_first,
    res_second,
    atom_proj,
    atom_self,
    atom_back,
):
    rows = edge_state[0, 0]
    edges, wide = rows.shape
    width = down_proj.shape[1]
    trips = trip_source.shape[2]

    far, own_w = pl.pallas_call(
        down_kernel,
        out_shape=(struct((FAR, edges // 2, 2 * width)), struct((2,) + res_first.shape)),
        in_specs=[VM] * 4,
        out_specs=(VM, VM),
        compiler_params=params(),
    )(rows, down_proj.T, res_first, res_second)

    groups = [
        [((z0 + 4 * i) % Z) * YH + h for i in range(4) for h in range(YH)] for z0 in range(4)
    ]
    near = lax.all_to_all(
        far, "src", split_axis=0, concat_axis=0, tiled=True, axis_index_groups=groups
    )
    x_w = [own_w] + [lax.ppermute(own_w, "tgt", along_x(d)) for d in (-1, 2, 1)]
    from_next = lax.ppermute(near, "src", shift(-1))
    from_prev = lax.ppermute(near, "src", shift(1))
    from_two = lax.ppermute(near, "src", shift_two())

    x_w = jnp.stack(x_w)
    y_w = lax.ppermute(x_w, "tgt", across(2))
    cx_w = lax.ppermute(x_w, "tgt", across(1))

    my_z = lax.axis_index("src") // YH
    ids = trip_source[0]
    q = ids >> 9
    zq = q >> 1
    pos = (((zq - my_z) & 3) * FAR + (zq >> 2) * 2 + (q & 1)) * (edges // 2) + (ids & 255)

    tm, send = pl.pallas_call(
        contract_kernel,
        out_shape=(struct((edges, width)), struct((NT, NT, 2 * width))),
        in_specs=[SM, SM] + [VM] * 8,
        out_specs=(VM, VM),
        scratch_shapes=[
            pltpu.VMEM((NS * edges // 2, 2 * width), F32),
            pltpu.VMEM((BLOCK, 2 * width), F32),
            pltpu.VMEM((BLOCK, 2 * width), F32),
            pltpu.VMEM((edges, 2 * width), F32),
            pltpu.VMEM((2 * width, edges), F32),
        ],
        compiler_params=params(),
    )(
        pos,
        trip_count,
        ids,
        trip_target[0],
        trip_basis[0, 0],
        bilinear.T,
        near,
        from_next,
        from_two,
        from_prev,
    )

    got = lax.all_to_all(send, "tgt", split_axis=0, concat_axis=0, tiled=True)
    got, y_w = lax.optimization_barrier((got, y_w))
    cy_w = lax.ppermute(y_w, "tgt", across(1))
    turned = pl.pallas_call(
        turn_kernel,
        out_shape=struct((NS, 8, 2 * width)),
        in_specs=[VM],
        out_specs=VM,
        scratch_shapes=[pltpu.VMEM((NT * NT, 2 * width), F32)],
        compiler_params=params(),
    )(got)
    arrived = lax.all_to_all(turned, "src", split_axis=0, concat_axis=0, tiled=True)

    atoms = atom_state.shape[1] * NT
    da = atom_state.shape[2]
    skipped, part = pl.pallas_call(
        edge_kernel,
        out_shape=(struct((edges, wide)), struct((atoms, da))),
        in_specs=[SM] + [VM] * 8 + [HB] * 4,
        out_specs=(VM, VM),
        scratch_shapes=[
            pltpu.VMEM((wide, wide), BF16),
            pltpu.VMEM((wide, wide), BF16),
            pltpu.SemaphoreType.DMA((2, NT)),
        ],
        compiler_params=params(),
    )(
        lax.axis_index("tgt").astype(jnp.int32).reshape(1, 1),
        rows,
        tm,
        arrived.reshape(edges // 2, 2 * width),
        reverse_perm[0],
        edge_source[0],
        up_forward,
        up_reverse,
        atom_proj,
        x_w,
        y_w,
        cx_w,
        cy_w,
    )

    parts = lax.all_to_all(
        part.reshape(NT, atoms // NT, da), "tgt", split_axis=0, concat_axis=0, tiled=True
    )
    atom_new, spread = pl.pallas_call(
        atom_kernel,
        out_shape=(struct((atoms // NT, da)), struct((NT, atoms // NT, da))),
        in_specs=[VM] * 3,
        out_specs=(VM, VM),
        compiler_params=params(),
    )(parts, atom_state[0], atom_self)
    block = lax.all_to_all(spread, "tgt", split_axis=0, concat_axis=0, tiled=True)
    edge_new = pl.pallas_call(
        final_kernel,
        out_shape=struct((edges, wide)),
        in_specs=[VM] * 4,
        out_specs=VM,
        compiler_params=params(),
    )(skipped, block.reshape(atoms, da), edge_source[0], atom_back)
    return (edge_new[None, None], atom_new[None])


def solution(mesh):
    return jax.shard_map(
        local,
        mesh=mesh,
        in_specs=(
            P("src", "tgt", None, None),
            P("src", "tgt", None),
            P("src", "tgt", None),
            P("src", "tgt", None),
            P("src", "tgt", None),
            P("src", "tgt"),
            P("src", "tgt", None, None),
            P("src", "tgt", None),
            P(),
            P(),
            P(),
            P(),
            P("tgt", None),
            P("tgt", None),
            P(),
            P(),
            P(),
        ),
        out_specs=(P("src", "tgt", None, None), P("src", "tgt", None)),
        check_vma=False,
    )
```

```python
import math

import jax
import jax.numpy as jnp
from jax import lax
from jax.experimental import pallas as pl
from jax.experimental.pallas import tpu as pltpu
from jax.sharding import PartitionSpec as P

INV_THREE = 1.0 / math.sqrt(3.0)
INV_TWO = 1.0 / math.sqrt(2.0)
F32 = jnp.float32
BF16 = jnp.bfloat16

Z, YH, NT = 16, 2, 16
NS = Z * YH
FAR = 8
NEAR = YH * NT
XS = 4
PEER = (0, 2, 1, 3)
BLOCK = 1024


def silu(v):
    return v * (0.5 * jnp.tanh(0.5 * v) + 0.5)


def dot(a, b, ca=1, cb=0):
    return lax.dot_general(a, b, (((ca,), (cb,)), ((), ())), preferred_element_type=F32)


def params(mb=48):
    return pltpu.CompilerParams(vmem_limit_bytes=mb * 1024 * 1024)


VM = pl.BlockSpec(memory_space=pltpu.VMEM)
SM = pl.BlockSpec(memory_space=pltpu.SMEM)
HB = pl.BlockSpec(memory_space=pl.ANY)


def down_kernel(x_ref, w_ref, o_ref, x, w, sems):
    load_w = pltpu.make_async_copy(w_ref, w, sems.at[0])
    load_x = pltpu.make_async_copy(x_ref, x, sems.at[1])
    load_w.start()
    load_x.start()
    load_w.wait()
    load_x.wait()
    y = silu(dot(x[...], w[...], 1, 1)).astype(BF16)
    half = y.shape[0] // 2
    packed = jnp.concatenate([y[:half], y[half:]], axis=1)
    for i in range(o_ref.shape[0]):
        o_ref[i] = packed


def pack_kernel(after_ref, a_ref, b_ref, ab_ref):
    ab_ref[0] = a_ref[...]
    ab_ref[1] = b_ref[...]


def contract_kernel(
    pos_ref, cnt_ref, ids_ref, tgt_ref, basis_ref, bil_ref, b0, b1, b2, b3,
    tm_ref, send_ref, col, rows_a, rows_b, acc, total,
):
    trips = tgt_ref.shape[1]
    edges, width = tm_ref.shape
    lanes = 2 * width
    step = rows_a.shape[0]

    def widen(i, c):
        for n, ref in enumerate((b0, b1, b2, b3)):
            at = pl.multiple_of((n * FAR + i) * 256, 256)
            col[pl.ds(at, 256), :] = ref[i].astype(F32)
        return c

    lax.fori_loop(0, FAR, widen, 0)

    count = cnt_ref[0, 0]
    nb = basis_ref.shape[0]
    eye = (
        lax.broadcasted_iota(jnp.int32, (lanes, lanes), 0)
        == lax.broadcasted_iota(jnp.int32, (lanes, lanes), 1)
    ).astype(BF16)
    edge_ids = lax.broadcasted_iota(jnp.int32, (edges, step), 0)
    slot_ids = lax.broadcasted_iota(jnp.int32, (1, step), 1)
    total[...] = jnp.zeros_like(total)

    def fetch(dst, at):
        for j in range(step):
            dst[j : j + 1, :] = col[pl.ds(pos_ref[0, at + j], 1), :]

    def block(at, rows):
        both = dot(eye, rows[...].astype(BF16), 1, 1)
        upper = ((ids_ref[:, at : at + step] >> 8) & 1) == 1
        msg = jnp.where(upper, both[width:], both[:width]).astype(BF16)
        basis = basis_ref[:, at : at + step]
        outer = jnp.concatenate([basis[c : c + 1, :] * msg for c in range(nb)], axis=0)
        out = dot(bil_ref[...], outer)
        hi = out.astype(BF16)
        lo = (out - hi.astype(F32)).astype(BF16)
        tgt = jnp.where(slot_ids + at < count, tgt_ref[:, at : at + step], -1)
        hot = jnp.where(edge_ids == tgt, 1.0, 0.0).astype(BF16)
        total[...] += dot(jnp.concatenate([hi, lo], axis=0), hot, 1, 1)

    held = (rows_a, rows_b)
    fetch(held[0], 0)
    for i in range(trips // step):
        if (i + 1) * step < trips:
            fetch(held[(i + 1) % 2], (i + 1) * step)
        block(i * step, held[i % 2])
    msg = jnp.transpose(total[:width, :] + total[width:, :]).astype(BF16)
    tm_ref[...] = msg
    acc[:, :width] = msg.astype(F32)
    for m in range(NEAR):
        first = acc[pl.ds(m, Z // 2, stride=NEAR), :]
        second = acc[pl.ds(NEAR * Z // 2 + m, Z // 2, stride=NEAR), :]
        send_ref[m] = jnp.concatenate([first[:, :width], second[:, :width]], axis=1).astype(BF16)


def turn_kernel(x_ref, o_ref, tmp):
    width = x_ref.shape[2] // 2
    half = Z // 2
    tmp[...] = x_ref[...].reshape(tmp.shape).astype(F32)
    for j in range(half):
        first = tmp[pl.ds(j, NEAR // 2, stride=half), :]
        second = tmp[pl.ds(NEAR // 2 * half + j, NEAR // 2, stride=half), :]
        o_ref[j] = jnp.concatenate([first[:, :width], second[:, :width]], axis=1).astype(BF16)
        o_ref[half + j] = jnp.concatenate([first[:, width:], second[:, width:]], axis=1).astype(BF16)


def edge_kernel(
    me_ref, x_ref, tm_ref, got_ref, perm_ref, src_ref, upf_ref, upr_ref, proj_ref,
    wa_ref, wb_ref, wc_ref, wd_ref, skip_ref, part_ref, w1, w2, sems,
):
    me = me_ref[0, 0]
    loads = ([], [])
    for k, w in enumerate((w1, w2)):
        for i, ref in enumerate((wa_ref, wb_ref, wc_ref, wd_ref)):
            for j in range(XS):
                at = (((((me >> 2) + j) & 3) * 4 + ((me & 3) ^ PEER[i]))) * ref.shape[2]
                at = pl.multiple_of(at, 64)
                loads[k].append(
                    pltpu.make_async_copy(
                        ref.at[j, k], w.at[pl.ds(at, ref.shape[2]), :], sems.at[k, i * XS + j]
                    )
                )
    for load in loads[0] + loads[1]:
        load.start()
    edges = x_ref.shape[0]
    width = tm_ref.shape[1]
    got = got_ref[...]
    got = jnp.concatenate([got[:, :width], got[:, width:]], axis=0)
    perm = perm_ref[...]
    row = ((perm >> 4) & 1) * (edges // 2) + (perm >> 5) * 16 + (perm & 15)
    hot = jnp.where(
        lax.broadcasted_iota(jnp.int32, (edges, edges), 0) == row, 1.0, 0.0
    ).astype(BF16)
    mirror_msg = dot(hot, got, 0, 0).astype(BF16)
    forward_out = silu(dot(tm_ref[...], upf_ref[...])).astype(BF16)
    mirrored = silu(dot(mirror_msg, upr_ref[...])).astype(BF16)
    mixed = (
        (x_ref[...].astype(F32) + forward_out.astype(F32) + mirrored.astype(F32)) * INV_THREE
    ).astype(BF16)
    for load in loads[0]:
        load.wait()
    inner = silu(dot(mixed, w1[...])).astype(BF16)
    for load in loads[1]:
        load.wait()
    skipped = ((mixed.astype(F32) + silu(dot(inner, w2[...]))) * INV_TWO).astype(BF16)
    skip_ref[...] = skipped
    terms = silu(dot(skipped, proj_ref[...])).astype(BF16)
    atoms = part_ref.shape[0]
    own = jnp.where(
        lax.broadcasted_iota(jnp.int32, (atoms, edges), 0) == src_ref[...], 1.0, 0.0
    ).astype(BF16)
    part_ref[...] = dot(own, terms).astype(BF16)


def atom_kernel(parts_ref, state_ref, w_ref, new_ref, send_ref):
    total = parts_ref[0].astype(F32)
    for i in range(1, NT):
        total = total + parts_ref[i].astype(F32)
    new = (state_ref[...].astype(F32) + silu(dot(total.astype(BF16), w_ref[...]))).astype(BF16)
    new_ref[...] = new
    for i in range(NT):
        send_ref[i] = new


def final_kernel(skip_ref, block_ref, src_ref, back_ref, o_ref):
    atoms = block_ref.shape[0]
    edges = skip_ref.shape[0]
    own = jnp.where(
        lax.broadcasted_iota(jnp.int32, (atoms, edges), 0) == src_ref[...], 1.0, 0.0
    ).astype(BF16)
    feats = dot(own, block_ref[...], 0, 0).astype(BF16)
    o_ref[...] = (skip_ref[...].astype(F32) + silu(dot(feats, back_ref[...]))).astype(BF16)


def shift(d):
    return [(z * YH + h, ((z + d) % Z) * YH + h) for z in range(Z) for h in range(YH)]


def shift_two():
    return [
        (z * YH + h, ((z + (2 if z % 2 == 0 else -2)) % Z) * YH + h)
        for z in range(Z)
        for h in range(YH)
    ]


def along_x(d):
    return [(t, ((t // 4 + d) % XS) * 4 + t % 4) for t in range(NT)]


def across(bit):
    return [(t, t ^ bit) for t in range(NT)]


def struct(shape, dtype=BF16):
    return jax.ShapeDtypeStruct(shape, dtype)


def local(
    edge_state,
    atom_state,
    edge_source,
    trip_source,
    trip_target,
    trip_count,
    trip_basis,
    reverse_perm,
    down_proj,
    bilinear,
    up_forward,
    up_reverse,
    res_first,
    res_second,
    atom_proj,
    atom_self,
    atom_back,
):
    rows = edge_state[0, 0]
    edges, wide = rows.shape
    width = down_proj.shape[1]
    trips = trip_source.shape[2]

    far = pl.pallas_call(
        down_kernel,
        out_shape=struct((FAR, edges // 2, 2 * width)),
        in_specs=[HB] * 2,
        out_specs=VM,
        scratch_shapes=[
            pltpu.VMEM((edges, wide), BF16),
            pltpu.VMEM((width, wide), BF16),
            pltpu.SemaphoreType.DMA((2,)),
        ],
        compiler_params=params(),
    )(rows, down_proj.T)

    groups = [
        [((z0 + 4 * i) % Z) * YH + h for i in range(4) for h in range(YH)] for z0 in range(4)
    ]
    near = lax.all_to_all(
        far, "src", split_axis=0, concat_axis=0, tiled=True, axis_index_groups=groups
    )
    own_w = pl.pallas_call(
        pack_kernel,
        out_shape=struct((2,) + res_first.shape),
        in_specs=[HB, VM, VM],
        out_specs=VM,
        compiler_params=params(),
    )(far, res_first, res_second)
    x_w = [own_w] + [lax.ppermute(own_w, "tgt", along_x(d)) for d in (-1, 2, 1)]
    from_next = lax.ppermute(near, "src", shift(-1))
    from_prev = lax.ppermute(near, "src", shift(1))
    from_two = lax.ppermute(near, "src", shift_two())

    x_w = jnp.stack(x_w)
    y_w = lax.ppermute(x_w, "tgt", across(2))
    cx_w = lax.ppermute(x_w, "tgt", across(1))

    my_z = lax.axis_index("src") // YH
    ids = trip_source[0]
    q = ids >> 9
    zq = q >> 1
    pos = (((zq - my_z) & 3) * FAR + (zq >> 2) * 2 + (q & 1)) * (edges // 2) + (ids & 255)

    tm, send = pl.pallas_call(
        contract_kernel,
        out_shape=(struct((edges, width)), struct((NEAR, Z // 2, 2 * width))),
        in_specs=[SM, SM] + [VM] * 8,
        out_specs=(VM, VM),
        scratch_shapes=[
            pltpu.VMEM((NS * edges // 2, 2 * width), F32),
            pltpu.VMEM((BLOCK, 2 * width), F32),
            pltpu.VMEM((BLOCK, 2 * width), F32),
            pltpu.VMEM((edges, 2 * width), F32),
            pltpu.VMEM((2 * width, edges), F32),
        ],
        compiler_params=params(),
        cost_estimate=pl.CostEstimate(flops=10**11, bytes_accessed=10**7, transcendentals=0),
    )(
        pos,
        trip_count,
        ids,
        trip_target[0],
        trip_basis[0, 0],
        bilinear.T,
        near,
        from_next,
        from_two,
        from_prev,
    )

    plane = [[(z * YH + h) * NT + t for h in range(YH) for t in range(NT)] for z in range(Z)]
    lines = [[z * YH + h for z in range(Z)] for h in range(YH)]
    got = lax.all_to_all(
        send, ("src", "tgt"), split_axis=0, concat_axis=0, tiled=True, axis_index_groups=plane
    )
    got, y_w = lax.optimization_barrier((got, y_w))
    cy_w = lax.ppermute(y_w, "tgt", across(1))
    turned = pl.pallas_call(
        turn_kernel,
        out_shape=struct((Z, NEAR // 2, 2 * width)),
        in_specs=[VM],
        out_specs=VM,
        scratch_shapes=[pltpu.VMEM((NEAR * Z // 2, 2 * width), F32)],
        compiler_params=params(),
    )(got)
    arrived = lax.all_to_all(
        turned, "src", split_axis=0, concat_axis=0, tiled=True, axis_index_groups=lines
    )

    atoms = atom_state.shape[1] * NT
    da = atom_state.shape[2]
    skipped, part = pl.pallas_call(
        edge_kernel,
        out_shape=(struct((edges, wide)), struct((atoms, da))),
        in_specs=[SM] + [VM] * 8 + [HB] * 4,
        out_specs=(VM, VM),
        scratch_shapes=[
            pltpu.VMEM((wide, wide), BF16),
            pltpu.VMEM((wide, wide), BF16),
            pltpu.SemaphoreType.DMA((2, NT)),
        ],
        compiler_params=params(),
    )(
        lax.axis_index("tgt").astype(jnp.int32).reshape(1, 1),
        rows,
        tm,
        arrived.reshape(edges // 2, 2 * width),
        reverse_perm[0],
        edge_source[0],
        up_forward,
        up_reverse,
        atom_proj,
        x_w,
        y_w,
        cx_w,
        cy_w,
    )

    parts = lax.all_to_all(
        part.reshape(NT, atoms // NT, da), "tgt", split_axis=0, concat_axis=0, tiled=True
    )
    atom_new, spread = pl.pallas_call(
        atom_kernel,
        out_shape=(struct((atoms // NT, da)), struct((NT, atoms // NT, da))),
        in_specs=[VM] * 3,
        out_specs=(VM, VM),
        compiler_params=params(),
    )(parts, atom_state[0], atom_self)
    block = lax.all_to_all(spread, "tgt", split_axis=0, concat_axis=0, tiled=True)
    edge_new = pl.pallas_call(
        final_kernel,
        out_shape=struct((edges, wide)),
        in_specs=[VM] * 4,
        out_specs=VM,
        compiler_params=params(),
    )(skipped, block.reshape(atoms, da), edge_source[0], atom_back)
    return (edge_new[None, None], atom_new[None])


def solution(mesh):
    return jax.shard_map(
        local,
        mesh=mesh,
        in_specs=(
            P("src", "tgt", None, None),
            P("src", "tgt", None),
            P("src", "tgt", None),
            P("src", "tgt", None),
            P("src", "tgt", None),
            P("src", "tgt"),
            P("src", "tgt", None, None),
            P("src", "tgt", None),
            P(),
            P(),
            P(),
            P(),
            P("tgt", None),
            P("tgt", None),
            P(),
            P(),
            P(),
        ),
        out_specs=(P("src", "tgt", None, None), P("src", "tgt", None)),
        check_vma=False,
    )
```

```python
import math

import jax
import jax.numpy as jnp
from jax import lax
from jax.experimental import pallas as pl
from jax.experimental.pallas import tpu as pltpu
from jax.sharding import PartitionSpec as P

INV_THREE = 1.0 / math.sqrt(3.0)
INV_TWO = 1.0 / math.sqrt(2.0)
F32 = jnp.float32
BF16 = jnp.bfloat16

Z, YH, NT = 16, 2, 16
NS = Z * YH
FAR = 8
NEAR = YH * NT
XS = 4
PEER = (0, 2, 1, 3)
BLOCK = 1024


def silu(v):
    return v * (0.5 * jnp.tanh(0.5 * v) + 0.5)


def dot(a, b, ca=1, cb=0):
    return lax.dot_general(a, b, (((ca,), (cb,)), ((), ())), preferred_element_type=F32)


def params(mb):
    return pltpu.CompilerParams(vmem_limit_bytes=mb * 1024 * 1024)


VM = pl.BlockSpec(memory_space=pltpu.VMEM)
SM = pl.BlockSpec(memory_space=pltpu.SMEM)
HB = pl.BlockSpec(memory_space=pl.ANY)


def down_kernel(x_ref, w_ref, o_ref, x, w, sems):
    load_w = pltpu.make_async_copy(w_ref, w, sems.at[0])
    load_x = pltpu.make_async_copy(x_ref, x, sems.at[1])
    load_w.start()
    load_x.start()
    load_w.wait()
    load_x.wait()
    y = silu(dot(x[...], w[...], 1, 1)).astype(BF16)
    half = y.shape[0] // 2
    packed = jnp.concatenate([y[:half], y[half:]], axis=1)
    for i in range(o_ref.shape[0]):
        o_ref[i] = packed


def pack_kernel(after_ref, a_ref, b_ref, ab_ref):
    ab_ref[0] = a_ref[...]
    ab_ref[1] = b_ref[...]


def contract_kernel(
    pos_ref, cnt_ref, ids_ref, tgt_ref, basis_ref, bil_ref, b0, b1, b2, b3,
    tm_ref, send_ref, col, rows_a, rows_b, acc, total,
):
    trips = tgt_ref.shape[1]
    edges, width = tm_ref.shape
    lanes = 2 * width
    step = rows_a.shape[0]

    def widen(i, c):
        for n, ref in enumerate((b0, b1, b2, b3)):
            at = pl.multiple_of((n * FAR + i) * 256, 256)
            col[pl.ds(at, 256), :] = ref[i].astype(F32)
        return c

    lax.fori_loop(0, FAR, widen, 0)

    count = cnt_ref[0, 0]
    nb = basis_ref.shape[0]
    eye = (
        lax.broadcasted_iota(jnp.int32, (lanes, lanes), 0)
        == lax.broadcasted_iota(jnp.int32, (lanes, lanes), 1)
    ).astype(BF16)
    edge_ids = lax.broadcasted_iota(jnp.int32, (edges, step), 0)
    slot_ids = lax.broadcasted_iota(jnp.int32, (1, step), 1)
    total[...] = jnp.zeros_like(total)

    def fetch(dst, at):
        for j in range(step):
            dst[j : j + 1, :] = col[pl.ds(pos_ref[0, at + j], 1), :]

    def block(at, rows):
        both = dot(eye, rows[...].astype(BF16), 1, 1)
        upper = ((ids_ref[:, at : at + step] >> 8) & 1) == 1
        msg = jnp.where(upper, both[width:], both[:width]).astype(BF16)
        basis = basis_ref[:, at : at + step]
        outer = jnp.concatenate([basis[c : c + 1, :] * msg for c in range(nb)], axis=0)
        out = dot(bil_ref[...], outer)
        hi = out.astype(BF16)
        lo = (out - hi.astype(F32)).astype(BF16)
        tgt = jnp.where(slot_ids + at < count, tgt_ref[:, at : at + step], -1)
        hot = jnp.where(edge_ids == tgt, 1.0, 0.0).astype(BF16)
        total[...] += dot(jnp.concatenate([hi, lo], axis=0), hot, 1, 1)

    held = (rows_a, rows_b)
    fetch(held[0], 0)
    for i in range(trips // step):
        if (i + 1) * step < trips:
            fetch(held[(i + 1) % 2], (i + 1) * step)
        block(i * step, held[i % 2])
    msg = jnp.transpose(total[:width, :] + total[width:, :]).astype(BF16)
    tm_ref[...] = msg
    acc[:, :width] = msg.astype(F32)
    for m in range(NEAR):
        first = acc[pl.ds(m, Z // 2, stride=NEAR), :]
        second = acc[pl.ds(NEAR * Z // 2 + m, Z // 2, stride=NEAR), :]
        send_ref[m] = jnp.concatenate([first[:, :width], second[:, :width]], axis=1).astype(BF16)


def turn_kernel(x_ref, o_ref, tmp):
    width = x_ref.shape[2] // 2
    half = Z // 2
    tmp[...] = x_ref[...].reshape(tmp.shape).astype(F32)
    for j in range(half):
        first = tmp[pl.ds(j, NEAR // 2, stride=half), :]
        second = tmp[pl.ds(NEAR // 2 * half + j, NEAR // 2, stride=half), :]
        o_ref[j] = jnp.concatenate([first[:, :width], second[:, :width]], axis=1).astype(BF16)
        o_ref[half + j] = jnp.concatenate([first[:, width:], second[:, width:]], axis=1).astype(BF16)


def forward_kernel(x_ref, tm_ref, upf_ref, o_ref):
    forward_out = silu(dot(tm_ref[...], upf_ref[...])).astype(BF16)
    o_ref[...] = x_ref[...].astype(F32) + forward_out.astype(F32)


def edge_kernel(
    me_ref, x_ref, got_ref, perm_ref, src_ref, upr_ref, proj_ref,
    wa_ref, wb_ref, wc_ref, wd_ref, skip_ref, part_ref, w1, w2, sems,
):
    me = me_ref[0, 0]
    loads = ([], [])
    for k, w in enumerate((w1, w2)):
        for i, ref in enumerate((wa_ref, wb_ref, wc_ref, wd_ref)):
            for j in range(XS):
                at = (((((me >> 2) + j) & 3) * 4 + ((me & 3) ^ PEER[i]))) * ref.shape[2]
                at = pl.multiple_of(at, 64)
                loads[k].append(
                    pltpu.make_async_copy(
                        ref.at[j, k], w.at[pl.ds(at, ref.shape[2]), :], sems.at[k, i * XS + j]
                    )
                )
    for load in loads[0] + loads[1]:
        load.start()
    edges = x_ref.shape[0]
    width = got_ref.shape[1] // 2
    got = got_ref[...]
    got = jnp.concatenate([got[:, :width], got[:, width:]], axis=0)
    perm = perm_ref[...]
    row = ((perm >> 4) & 1) * (edges // 2) + (perm >> 5) * 16 + (perm & 15)
    hot = jnp.where(
        lax.broadcasted_iota(jnp.int32, (edges, edges), 0) == row, 1.0, 0.0
    ).astype(BF16)
    mirror_msg = dot(hot, got, 0, 0).astype(BF16)
    mirrored = silu(dot(mirror_msg, upr_ref[...])).astype(BF16)
    mixed = ((x_ref[...] + mirrored.astype(F32)) * INV_THREE).astype(BF16)
    for load in loads[0]:
        load.wait()
    inner = silu(dot(mixed, w1[...])).astype(BF16)
    for load in loads[1]:
        load.wait()
    skipped = ((mixed.astype(F32) + silu(dot(inner, w2[...]))) * INV_TWO).astype(BF16)
    skip_ref[...] = skipped
    terms = silu(dot(skipped, proj_ref[...])).astype(BF16)
    atoms = part_ref.shape[0]
    own = jnp.where(
        lax.broadcasted_iota(jnp.int32, (atoms, edges), 0) == src_ref[...], 1.0, 0.0
    ).astype(BF16)
    part_ref[...] = dot(own, terms).astype(BF16)


def atom_kernel(parts_ref, state_ref, w_ref, new_ref, send_ref):
    total = parts_ref[0].astype(F32)
    for i in range(1, NT):
        total = total + parts_ref[i].astype(F32)
    new = (state_ref[...].astype(F32) + silu(dot(total.astype(BF16), w_ref[...]))).astype(BF16)
    new_ref[...] = new
    for i in range(NT):
        send_ref[i] = new


def final_kernel(skip_ref, block_ref, src_ref, back_ref, o_ref):
    atoms = block_ref.shape[0]
    edges = skip_ref.shape[0]
    own = jnp.where(
        lax.broadcasted_iota(jnp.int32, (atoms, edges), 0) == src_ref[...], 1.0, 0.0
    ).astype(BF16)
    feats = dot(own, block_ref[...], 0, 0).astype(BF16)
    o_ref[...] = (skip_ref[...].astype(F32) + silu(dot(feats, back_ref[...]))).astype(BF16)


def shift(d):
    return [(z * YH + h, ((z + d) % Z) * YH + h) for z in range(Z) for h in range(YH)]


def shift_two():
    return [
        (z * YH + h, ((z + (2 if z % 2 == 0 else -2)) % Z) * YH + h)
        for z in range(Z)
        for h in range(YH)
    ]


def along_x(d):
    return [(t, ((t // 4 + d) % XS) * 4 + t % 4) for t in range(NT)]


def across(bit):
    return [(t, t ^ bit) for t in range(NT)]


def struct(shape, dtype=BF16):
    return jax.ShapeDtypeStruct(shape, dtype)


def local(
    edge_state,
    atom_state,
    edge_source,
    trip_source,
    trip_target,
    trip_count,
    trip_basis,
    reverse_perm,
    down_proj,
    bilinear,
    up_forward,
    up_reverse,
    res_first,
    res_second,
    atom_proj,
    atom_self,
    atom_back,
):
    rows = edge_state[0, 0]
    edges, wide = rows.shape
    width = down_proj.shape[1]
    trips = trip_source.shape[2]

    far = pl.pallas_call(
        down_kernel,
        out_shape=struct((FAR, edges // 2, 2 * width)),
        in_specs=[HB] * 2,
        out_specs=VM,
        scratch_shapes=[
            pltpu.VMEM((edges, wide), BF16),
            pltpu.VMEM((width, wide), BF16),
            pltpu.SemaphoreType.DMA((2,)),
        ],
        compiler_params=params(60),
    )(rows, down_proj.T)

    groups = [
        [((z0 + 4 * i) % Z) * YH + h for i in range(4) for h in range(YH)] for z0 in range(4)
    ]
    near = lax.all_to_all(
        far, "src", split_axis=0, concat_axis=0, tiled=True, axis_index_groups=groups
    )
    own_w = pl.pallas_call(
        pack_kernel,
        out_shape=struct((2,) + res_first.shape),
        in_specs=[HB, VM, VM],
        out_specs=VM,
        compiler_params=params(4),
    )(far, res_first, res_second)
    x_w = [own_w] + [lax.ppermute(own_w, "tgt", along_x(d)) for d in (-1, 2, 1)]
    from_next = lax.ppermute(near, "src", shift(-1))
    from_prev = lax.ppermute(near, "src", shift(1))
    from_two = lax.ppermute(near, "src", shift_two())

    x_w = jnp.stack(x_w)
    y_w = lax.ppermute(x_w, "tgt", across(2))

    my_z = lax.axis_index("src") // YH
    ids = trip_source[0]
    q = ids >> 9
    zq = q >> 1
    pos = (((zq - my_z) & 3) * FAR + (zq >> 2) * 2 + (q & 1)) * (edges // 2) + (ids & 255)

    tm, send = pl.pallas_call(
        contract_kernel,
        out_shape=(struct((edges, width)), struct((NEAR, Z // 2, 2 * width))),
        in_specs=[SM, SM] + [VM] * 8,
        out_specs=(VM, VM),
        scratch_shapes=[
            pltpu.VMEM((NS * edges // 2, 2 * width), F32),
            pltpu.VMEM((BLOCK, 2 * width), F32),
            pltpu.VMEM((BLOCK, 2 * width), F32),
            pltpu.VMEM((edges, 2 * width), F32),
            pltpu.VMEM((2 * width, edges), F32),
        ],
        compiler_params=params(24),
        cost_estimate=pl.CostEstimate(flops=10**11, bytes_accessed=10**7, transcendentals=0),
    )(
        pos,
        trip_count,
        ids,
        trip_target[0],
        trip_basis[0, 0],
        bilinear.T,
        near,
        from_next,
        from_two,
        from_prev,
    )

    plane = [[(z * YH + h) * NT + t for h in range(YH) for t in range(NT)] for z in range(Z)]
    lines = [[z * YH + h for z in range(Z)] for h in range(YH)]
    got = lax.all_to_all(
        send, ("src", "tgt"), split_axis=0, concat_axis=0, tiled=True, axis_index_groups=plane
    )
    turned = pl.pallas_call(
        turn_kernel,
        out_shape=struct((Z, NEAR // 2, 2 * width)),
        in_specs=[VM],
        out_specs=VM,
        scratch_shapes=[pltpu.VMEM((NEAR * Z // 2, 2 * width), F32)],
        compiler_params=params(4),
    )(got)
    turned, x_w, y_w = lax.optimization_barrier((turned, x_w, y_w))
    cx_w = lax.ppermute(x_w, "tgt", across(1))
    cy_w = lax.ppermute(y_w, "tgt", across(1))
    arrived = lax.all_to_all(
        turned, "src", split_axis=0, concat_axis=0, tiled=True, axis_index_groups=lines
    )

    atoms = atom_state.shape[1] * NT
    da = atom_state.shape[2]
    base = pl.pallas_call(
        forward_kernel,
        out_shape=struct((edges, wide), F32),
        in_specs=[VM] * 3,
        out_specs=VM,
        compiler_params=params(12),
        cost_estimate=pl.CostEstimate(flops=10**11, bytes_accessed=10**6, transcendentals=0),
    )(rows, tm, up_forward)
    skipped, part = pl.pallas_call(
        edge_kernel,
        out_shape=(struct((edges, wide)), struct((atoms, da))),
        in_specs=[SM] + [VM] * 6 + [HB] * 4,
        out_specs=(VM, VM),
        scratch_shapes=[
            pltpu.VMEM((wide, wide), BF16),
            pltpu.VMEM((wide, wide), BF16),
            pltpu.SemaphoreType.DMA((2, NT)),
        ],
        compiler_params=params(20),
    )(
        lax.axis_index("tgt").astype(jnp.int32).reshape(1, 1),
        base,
        arrived.reshape(edges // 2, 2 * width),
        reverse_perm[0],
        edge_source[0],
        up_reverse,
        atom_proj,
        x_w,
        y_w,
        cx_w,
        cy_w,
    )

    parts = lax.all_to_all(
        part.reshape(NT, atoms // NT, da), "tgt", split_axis=0, concat_axis=0, tiled=True
    )
    atom_new, spread = pl.pallas_call(
        atom_kernel,
        out_shape=(struct((atoms // NT, da)), struct((NT, atoms // NT, da))),
        in_specs=[VM] * 3,
        out_specs=(VM, VM),
        compiler_params=params(4),
    )(parts, atom_state[0], atom_self)
    block = lax.all_to_all(spread, "tgt", split_axis=0, concat_axis=0, tiled=True)
    edge_new = pl.pallas_call(
        final_kernel,
        out_shape=struct((edges, wide)),
        in_specs=[VM] * 4,
        out_specs=VM,
        compiler_params=params(8),
    )(skipped, block.reshape(atoms, da), edge_source[0], atom_back)
    return (edge_new[None, None], atom_new[None])


def solution(mesh):
    return jax.shard_map(
        local,
        mesh=mesh,
        in_specs=(
            P("src", "tgt", None, None),
            P("src", "tgt", None),
            P("src", "tgt", None),
            P("src", "tgt", None),
            P("src", "tgt", None),
            P("src", "tgt"),
            P("src", "tgt", None, None),
            P("src", "tgt", None),
            P(),
            P(),
            P(),
            P(),
            P("tgt", None),
            P("tgt", None),
            P(),
            P(),
            P(),
        ),
        out_specs=(P("src", "tgt", None, None), P("src", "tgt", None)),
        check_vma=False,
    )
```

```python
import math

import jax
import jax.numpy as jnp
from jax import lax
from jax.experimental import pallas as pl
from jax.experimental.pallas import tpu as pltpu
from jax.sharding import PartitionSpec as P

INV_THREE = 1.0 / math.sqrt(3.0)
INV_TWO = 1.0 / math.sqrt(2.0)
F32 = jnp.float32
BF16 = jnp.bfloat16

Z, YH, NT = 16, 2, 16
NS = Z * YH
FAR = 4
NEAR = YH * NT
XS = 4
PEER = (0, 2, 1, 3)
BLOCK = 1024


def silu(v):
    return v * (0.5 * jnp.tanh(0.5 * v) + 0.5)


def dot(a, b, ca=1, cb=0):
    return lax.dot_general(a, b, (((ca,), (cb,)), ((), ())), preferred_element_type=F32)


def params(mb):
    return pltpu.CompilerParams(vmem_limit_bytes=mb * 1024 * 1024)


VM = pl.BlockSpec(memory_space=pltpu.VMEM)
SM = pl.BlockSpec(memory_space=pltpu.SMEM)
HB = pl.BlockSpec(memory_space=pl.ANY)


def down_kernel(x_ref, w_ref, o_ref, x, w, sems):
    load_w = pltpu.make_async_copy(w_ref, w, sems.at[0])
    load_x = pltpu.make_async_copy(x_ref, x, sems.at[1])
    load_w.start()
    load_x.start()
    load_w.wait()
    load_x.wait()
    y = silu(dot(x[...], w[...], 1, 1)).astype(BF16)
    half = y.shape[0] // 2
    packed = jnp.concatenate([y[:half], y[half:]], axis=1)
    for i in range(o_ref.shape[0]):
        o_ref[i] = packed


def pack_kernel(after_ref, a_ref, b_ref, ab_ref):
    ab_ref[0] = a_ref[...]
    ab_ref[1] = b_ref[...]


def contract_kernel(
    pos_ref, cnt_ref, ids_ref, tgt_ref, basis_ref, bil_ref, b0, b1, b2, b3, c0, c1, c2, c3,
    tm_ref, send_ref, col, rows_a, rows_b, acc, total,
):
    trips = tgt_ref.shape[1]
    edges, width = tm_ref.shape
    lanes = 2 * width
    step = rows_a.shape[0]

    def widen(i, c):
        for n, ref in enumerate((b0, b1, b2, b3, c0, c1, c2, c3)):
            at = pl.multiple_of((n * FAR + i) * 256, 256)
            col[pl.ds(at, 256), :] = ref[i].astype(F32)
        return c

    lax.fori_loop(0, FAR, widen, 0)

    count = cnt_ref[0, 0]
    nb = basis_ref.shape[0]
    eye = (
        lax.broadcasted_iota(jnp.int32, (lanes, lanes), 0)
        == lax.broadcasted_iota(jnp.int32, (lanes, lanes), 1)
    ).astype(BF16)
    edge_ids = lax.broadcasted_iota(jnp.int32, (edges, step), 0)
    slot_ids = lax.broadcasted_iota(jnp.int32, (1, step), 1)
    total[...] = jnp.zeros_like(total)

    def fetch(dst, at):
        for j in range(step):
            dst[j : j + 1, :] = col[pl.ds(pos_ref[0, at + j], 1), :]

    def block(at, rows):
        both = dot(eye, rows[...].astype(BF16), 1, 1)
        upper = ((ids_ref[:, at : at + step] >> 8) & 1) == 1
        msg = jnp.where(upper, both[width:], both[:width]).astype(BF16)
        basis = basis_ref[:, at : at + step]
        outer = jnp.concatenate([basis[c : c + 1, :] * msg for c in range(nb)], axis=0)
        out = dot(bil_ref[...], outer)
        hi = out.astype(BF16)
        lo = (out - hi.astype(F32)).astype(BF16)
        tgt = jnp.where(slot_ids + at < count, tgt_ref[:, at : at + step], -1)
        hot = jnp.where(edge_ids == tgt, 1.0, 0.0).astype(BF16)
        total[...] += dot(jnp.concatenate([hi, lo], axis=0), hot, 1, 1)

    held = (rows_a, rows_b)
    fetch(held[0], 0)
    for i in range(trips // step):
        if (i + 1) * step < trips:
            fetch(held[(i + 1) % 2], (i + 1) * step)
        block(i * step, held[i % 2])
    msg = jnp.transpose(total[:width, :] + total[width:, :]).astype(BF16)
    tm_ref[...] = msg
    acc[:, :width] = msg.astype(F32)
    for m in range(NEAR):
        first = acc[pl.ds(m, Z // 2, stride=NEAR), :]
        second = acc[pl.ds(NEAR * Z // 2 + m, Z // 2, stride=NEAR), :]
        send_ref[m] = jnp.concatenate([first[:, :width], second[:, :width]], axis=1).astype(BF16)


def turn_kernel(x_ref, o_ref, tmp):
    width = x_ref.shape[2] // 2
    half = Z // 2
    tmp[...] = x_ref[...].reshape(tmp.shape).astype(F32)
    for j in range(half):
        first = tmp[pl.ds(j, NEAR // 2, stride=half), :]
        second = tmp[pl.ds(NEAR // 2 * half + j, NEAR // 2, stride=half), :]
        o_ref[j] = jnp.concatenate([first[:, :width], second[:, :width]], axis=1).astype(BF16)
        o_ref[half + j] = jnp.concatenate([first[:, width:], second[:, width:]], axis=1).astype(BF16)


def forward_kernel(x_ref, tm_ref, upf_ref, o_ref):
    forward_out = silu(dot(tm_ref[...], upf_ref[...])).astype(BF16)
    o_ref[...] = x_ref[...].astype(F32) + forward_out.astype(F32)


def edge_kernel(
    me_ref, x_ref, got_ref, perm_ref, src_ref, upr_ref, proj_ref,
    wa_ref, wb_ref, wc_ref, wd_ref, skip_ref, part_ref, w1, w2, sems,
):
    me = me_ref[0, 0]
    loads = ([], [])
    for k, w in enumerate((w1, w2)):
        for i, ref in enumerate((wa_ref, wb_ref, wc_ref, wd_ref)):
            for j in range(XS):
                at = (((((me >> 2) + j) & 3) * 4 + ((me & 3) ^ PEER[i]))) * ref.shape[2]
                at = pl.multiple_of(at, 64)
                loads[k].append(
                    pltpu.make_async_copy(
                        ref.at[j, k], w.at[pl.ds(at, ref.shape[2]), :], sems.at[k, i * XS + j]
                    )
                )
    for load in loads[0] + loads[1]:
        load.start()
    edges = x_ref.shape[0]
    width = got_ref.shape[1] // 2
    got = got_ref[...]
    got = jnp.concatenate([got[:, :width], got[:, width:]], axis=0)
    perm = perm_ref[...]
    row = ((perm >> 4) & 1) * (edges // 2) + (perm >> 5) * 16 + (perm & 15)
    hot = jnp.where(
        lax.broadcasted_iota(jnp.int32, (edges, edges), 0) == row, 1.0, 0.0
    ).astype(BF16)
    mirror_msg = dot(hot, got, 0, 0).astype(BF16)
    mirrored = silu(dot(mirror_msg, upr_ref[...])).astype(BF16)
    mixed = ((x_ref[...] + mirrored.astype(F32)) * INV_THREE).astype(BF16)
    for load in loads[0]:
        load.wait()
    inner = silu(dot(mixed, w1[...])).astype(BF16)
    for load in loads[1]:
        load.wait()
    skipped = ((mixed.astype(F32) + silu(dot(inner, w2[...]))) * INV_TWO).astype(BF16)
    skip_ref[...] = skipped
    terms = silu(dot(skipped, proj_ref[...])).astype(BF16)
    atoms = part_ref.shape[0]
    own = jnp.where(
        lax.broadcasted_iota(jnp.int32, (atoms, edges), 0) == src_ref[...], 1.0, 0.0
    ).astype(BF16)
    part_ref[...] = dot(own, terms).astype(BF16)


def atom_kernel(parts_ref, state_ref, w_ref, new_ref, send_ref):
    total = parts_ref[0].astype(F32)
    for i in range(1, NT):
        total = total + parts_ref[i].astype(F32)
    new = (state_ref[...].astype(F32) + silu(dot(total.astype(BF16), w_ref[...]))).astype(BF16)
    new_ref[...] = new
    for i in range(NT):
        send_ref[i] = new


def final_kernel(skip_ref, block_ref, src_ref, back_ref, o_ref):
    atoms = block_ref.shape[0]
    edges = skip_ref.shape[0]
    own = jnp.where(
        lax.broadcasted_iota(jnp.int32, (atoms, edges), 0) == src_ref[...], 1.0, 0.0
    ).astype(BF16)
    feats = dot(own, block_ref[...], 0, 0).astype(BF16)
    o_ref[...] = (skip_ref[...].astype(F32) + silu(dot(feats, back_ref[...]))).astype(BF16)


def shift(d):
    return [(z * YH + h, ((z + d) % Z) * YH + h) for z in range(Z) for h in range(YH)]


def swap():
    return [(i, i ^ 1) for i in range(NS)]


def shift_two():
    return [
        (z * YH + h, ((z + (2 if z % 2 == 0 else -2)) % Z) * YH + h)
        for z in range(Z)
        for h in range(YH)
    ]


def along_x(d):
    return [(t, ((t // 4 + d) % XS) * 4 + t % 4) for t in range(NT)]


def across(bit):
    return [(t, t ^ bit) for t in range(NT)]


def struct(shape, dtype=BF16):
    return jax.ShapeDtypeStruct(shape, dtype)


def local(
    edge_state,
    atom_state,
    edge_source,
    trip_source,
    trip_target,
    trip_count,
    trip_basis,
    reverse_perm,
    down_proj,
    bilinear,
    up_forward,
    up_reverse,
    res_first,
    res_second,
    atom_proj,
    atom_self,
    atom_back,
):
    rows = edge_state[0, 0]
    edges, wide = rows.shape
    width = down_proj.shape[1]
    trips = trip_source.shape[2]

    far = pl.pallas_call(
        down_kernel,
        out_shape=struct((FAR, edges // 2, 2 * width)),
        in_specs=[HB] * 2,
        out_specs=VM,
        scratch_shapes=[
            pltpu.VMEM((edges, wide), BF16),
            pltpu.VMEM((width, wide), BF16),
            pltpu.SemaphoreType.DMA((2,)),
        ],
        compiler_params=params(60),
    )(rows, down_proj.T)

    groups = [[((z0 + 4 * i) % Z) * YH + h for i in range(4)] for z0 in range(4) for h in range(YH)]
    own = lax.all_to_all(
        far, "src", split_axis=0, concat_axis=0, tiled=True, axis_index_groups=groups
    )
    other = lax.ppermute(own, "src", swap())
    own_w = pl.pallas_call(
        pack_kernel,
        out_shape=struct((2,) + res_first.shape),
        in_specs=[HB, VM, VM],
        out_specs=VM,
        compiler_params=params(4),
    )(far, res_first, res_second)
    x_w = [own_w] + [lax.ppermute(own_w, "tgt", along_x(d)) for d in (-1, 2, 1)]
    pieces = []
    for part in (own, other):
        pieces += [part] + [lax.ppermute(part, "src", p) for p in (shift(-1), shift_two(), shift(1))]
    x_w = jnp.stack(x_w)
    y_w = lax.ppermute(x_w, "tgt", across(2))

    my_z = lax.axis_index("src") // YH
    ids = trip_source[0]
    q = ids >> 9
    zq = q >> 1
    other_y = (q ^ lax.axis_index("src")) & 1
    pos = ((other_y * 4 + ((zq - my_z) & 3)) * FAR + (zq >> 2)) * (edges // 2) + (ids & 255)

    tm, send = pl.pallas_call(
        contract_kernel,
        out_shape=(struct((edges, width)), struct((NEAR, Z // 2, 2 * width))),
        in_specs=[SM, SM] + [VM] * 12,
        out_specs=(VM, VM),
        scratch_shapes=[
            pltpu.VMEM((NS * edges // 2, 2 * width), F32),
            pltpu.VMEM((BLOCK, 2 * width), F32),
            pltpu.VMEM((BLOCK, 2 * width), F32),
            pltpu.VMEM((edges, 2 * width), F32),
            pltpu.VMEM((2 * width, edges), F32),
        ],
        compiler_params=params(24),
        cost_estimate=pl.CostEstimate(flops=10**11, bytes_accessed=10**7, transcendentals=0),
    )(
        pos,
        trip_count,
        ids,
        trip_target[0],
        trip_basis[0, 0],
        bilinear.T,
        *pieces,
    )

    plane = [[(z * YH + h) * NT + t for h in range(YH) for t in range(NT)] for z in range(Z)]
    lines = [[z * YH + h for z in range(Z)] for h in range(YH)]
    got = lax.all_to_all(
        send, ("src", "tgt"), split_axis=0, concat_axis=0, tiled=True, axis_index_groups=plane
    )
    turned = pl.pallas_call(
        turn_kernel,
        out_shape=struct((Z, NEAR // 2, 2 * width)),
        in_specs=[VM],
        out_specs=VM,
        scratch_shapes=[pltpu.VMEM((NEAR * Z // 2, 2 * width), F32)],
        compiler_params=params(4),
    )(got)
    turned, x_w, y_w = lax.optimization_barrier((turned, x_w, y_w))
    cx_w = lax.ppermute(x_w, "tgt", across(1))
    cy_w = lax.ppermute(y_w, "tgt", across(1))
    arrived = lax.all_to_all(
        turned, "src", split_axis=0, concat_axis=0, tiled=True, axis_index_groups=lines
    )

    atoms = atom_state.shape[1] * NT
    da = atom_state.shape[2]
    base = pl.pallas_call(
        forward_kernel,
        out_shape=struct((edges, wide), F32),
        in_specs=[VM] * 3,
        out_specs=VM,
        compiler_params=params(12),
        cost_estimate=pl.CostEstimate(flops=10**11, bytes_accessed=10**6, transcendentals=0),
    )(rows, tm, up_forward)
    skipped, part = pl.pallas_call(
        edge_kernel,
        out_shape=(struct((edges, wide)), struct((atoms, da))),
        in_specs=[SM] + [VM] * 6 + [HB] * 4,
        out_specs=(VM, VM),
        scratch_shapes=[
            pltpu.VMEM((wide, wide), BF16),
            pltpu.VMEM((wide, wide), BF16),
            pltpu.SemaphoreType.DMA((2, NT)),
        ],
        compiler_params=params(20),
    )(
        lax.axis_index("tgt").astype(jnp.int32).reshape(1, 1),
        base,
        arrived.reshape(edges // 2, 2 * width),
        reverse_perm[0],
        edge_source[0],
        up_reverse,
        atom_proj,
        x_w,
        y_w,
        cx_w,
        cy_w,
    )

    parts = lax.all_to_all(
        part.reshape(NT, atoms // NT, da), "tgt", split_axis=0, concat_axis=0, tiled=True
    )
    atom_new, spread = pl.pallas_call(
        atom_kernel,
        out_shape=(struct((atoms // NT, da)), struct((NT, atoms // NT, da))),
        in_specs=[VM] * 3,
        out_specs=(VM, VM),
        compiler_params=params(4),
    )(parts, atom_state[0], atom_self)
    block = lax.all_to_all(spread, "tgt", split_axis=0, concat_axis=0, tiled=True)
    edge_new = pl.pallas_call(
        final_kernel,
        out_shape=struct((edges, wide)),
        in_specs=[VM] * 4,
        out_specs=VM,
        compiler_params=params(8),
    )(skipped, block.reshape(atoms, da), edge_source[0], atom_back)
    return (edge_new[None, None], atom_new[None])


def solution(mesh):
    return jax.shard_map(
        local,
        mesh=mesh,
        in_specs=(
            P("src", "tgt", None, None),
            P("src", "tgt", None),
            P("src", "tgt", None),
            P("src", "tgt", None),
            P("src", "tgt", None),
            P("src", "tgt"),
            P("src", "tgt", None, None),
            P("src", "tgt", None),
            P(),
            P(),
            P(),
            P(),
            P("tgt", None),
            P("tgt", None),
            P(),
            P(),
            P(),
        ),
        out_specs=(P("src", "tgt", None, None), P("src", "tgt", None)),
        check_vma=False,
    )
```

```python
import math

import jax
import jax.numpy as jnp
from jax import lax
from jax.experimental import pallas as pl
from jax.experimental.pallas import tpu as pltpu
from jax.sharding import PartitionSpec as P

INV_THREE = 1.0 / math.sqrt(3.0)
INV_TWO = 1.0 / math.sqrt(2.0)
F32 = jnp.float32
BF16 = jnp.bfloat16

Z, YH, NT = 16, 2, 16
NS = Z * YH
FAR = 4
NEAR = YH * NT
XS = 4
PEER = (0, 2, 1, 3)
BLOCK = 2048


def silu(v):
    return v * (0.5 * jnp.tanh(0.5 * v) + 0.5)


def dot(a, b, ca=1, cb=0):
    return lax.dot_general(a, b, (((ca,), (cb,)), ((), ())), preferred_element_type=F32)


def params(mb):
    return pltpu.CompilerParams(vmem_limit_bytes=mb * 1024 * 1024)


VM = pl.BlockSpec(memory_space=pltpu.VMEM)
SM = pl.BlockSpec(memory_space=pltpu.SMEM)
HB = pl.BlockSpec(memory_space=pl.ANY)


def down_kernel(x_ref, w_ref, o_ref, x, w, sems):
    load_w = pltpu.make_async_copy(w_ref, w, sems.at[0])
    load_w.start()
    half = x.shape[0] // 2
    step = half // 2
    loads = []
    for i in range(2):
        for side in range(2):
            at = pl.ds(side * half + i * step, step)
            loads.append(pltpu.make_async_copy(x_ref.at[at], x.at[at], sems.at[1 + len(loads)]))
            loads[-1].start()
    load_w.wait()
    for i in range(2):
        parts = []
        for side in range(2):
            loads[i * 2 + side].wait()
            rows = x[pl.ds(side * half + i * step, step), :]
            parts.append(silu(dot(rows, w[...], 1, 1)).astype(BF16))
        packed = jnp.concatenate(parts, axis=1)
        for k in range(o_ref.shape[0]):
            o_ref[k, pl.ds(i * step, step), :] = packed


def pack_kernel(after_ref, a_ref, b_ref, ab_ref):
    ab_ref[0] = a_ref[...]
    ab_ref[1] = b_ref[...]


def contract_kernel(
    pos_ref, cnt_ref, ids_ref, tgt_ref, basis_ref, bil_ref, b0, b1, b2, b3, c0, c1, c2, c3,
    tm_ref, send_ref, col, rows_a, rows_b, acc, total,
):
    trips = tgt_ref.shape[1]
    edges, width = tm_ref.shape
    lanes = 2 * width
    step = rows_a.shape[0]

    def widen(i, c):
        for n, ref in enumerate((b0, b1, b2, b3, c0, c1, c2, c3)):
            at = pl.multiple_of((n * FAR + i) * 256, 256)
            col[pl.ds(at, 256), :] = ref[i].astype(F32)
        return c

    lax.fori_loop(0, FAR, widen, 0)

    count = cnt_ref[0, 0]
    nb = basis_ref.shape[0]
    eye = (
        lax.broadcasted_iota(jnp.int32, (lanes, lanes), 0)
        == lax.broadcasted_iota(jnp.int32, (lanes, lanes), 1)
    ).astype(BF16)
    edge_ids = lax.broadcasted_iota(jnp.int32, (edges, step), 0)
    slot_ids = lax.broadcasted_iota(jnp.int32, (1, step), 1)
    total[...] = jnp.zeros_like(total)

    def fetch(dst, at):
        for j in range(step):
            dst[j : j + 1, :] = col[pl.ds(pos_ref[0, at + j], 1), :]

    def block(at, rows):
        both = dot(eye, rows[...].astype(BF16), 1, 1)
        upper = ((ids_ref[:, at : at + step] >> 8) & 1) == 1
        msg = jnp.where(upper, both[width:], both[:width]).astype(BF16)
        basis = basis_ref[:, at : at + step]
        outer = jnp.concatenate([basis[c : c + 1, :] * msg for c in range(nb)], axis=0)
        out = dot(bil_ref[...], outer)
        hi = out.astype(BF16)
        lo = (out - hi.astype(F32)).astype(BF16)
        tgt = jnp.where(slot_ids + at < count, tgt_ref[:, at : at + step], -1)
        hot = jnp.where(edge_ids == tgt, 1.0, 0.0).astype(BF16)
        total[...] += dot(jnp.concatenate([hi, lo], axis=0), hot, 1, 1)

    held = (rows_a, rows_b)
    fetch(held[0], 0)
    for i in range(trips // step):
        if (i + 1) * step < trips:
            fetch(held[(i + 1) % 2], (i + 1) * step)
        block(i * step, held[i % 2])
    msg = jnp.transpose(total[:width, :] + total[width:, :]).astype(BF16)
    tm_ref[...] = msg
    acc[:, :width] = msg.astype(F32)
    for m in range(NEAR):
        first = acc[pl.ds(m, Z // 2, stride=NEAR), :]
        second = acc[pl.ds(NEAR * Z // 2 + m, Z // 2, stride=NEAR), :]
        send_ref[m] = jnp.concatenate([first[:, :width], second[:, :width]], axis=1).astype(BF16)


def turn_kernel(x_ref, o_ref, tmp):
    width = x_ref.shape[2] // 2
    half = Z // 2
    tmp[...] = x_ref[...].reshape(tmp.shape).astype(F32)
    for j in range(half):
        first = tmp[pl.ds(j, NEAR // 2, stride=half), :]
        second = tmp[pl.ds(NEAR // 2 * half + j, NEAR // 2, stride=half), :]
        o_ref[j] = jnp.concatenate([first[:, :width], second[:, :width]], axis=1).astype(BF16)
        o_ref[half + j] = jnp.concatenate([first[:, width:], second[:, width:]], axis=1).astype(BF16)


def forward_kernel(x_ref, tm_ref, upf_ref, o_ref):
    forward_out = silu(dot(tm_ref[...], upf_ref[...])).astype(BF16)
    o_ref[...] = x_ref[...].astype(F32) + forward_out.astype(F32)


def edge_kernel(
    me_ref, x_ref, got_ref, perm_ref, src_ref, upr_ref, proj_ref,
    wa_ref, wb_ref, wc_ref, wd_ref, skip_ref, part_ref, w1, w2, sems,
):
    me = me_ref[0, 0]
    loads = ([], [])
    for k, w in enumerate((w1, w2)):
        for i, ref in enumerate((wa_ref, wb_ref, wc_ref, wd_ref)):
            for j in range(XS):
                at = (((((me >> 2) + j) & 3) * 4 + ((me & 3) ^ PEER[i]))) * ref.shape[2]
                at = pl.multiple_of(at, 64)
                loads[k].append(
                    pltpu.make_async_copy(
                        ref.at[j, k], w.at[pl.ds(at, ref.shape[2]), :], sems.at[k, i * XS + j]
                    )
                )
    for load in loads[0] + loads[1]:
        load.start()
    edges = x_ref.shape[0]
    width = got_ref.shape[1] // 2
    got = got_ref[...]
    got = jnp.concatenate([got[:, :width], got[:, width:]], axis=0)
    perm = perm_ref[...]
    row = ((perm >> 4) & 1) * (edges // 2) + (perm >> 5) * 16 + (perm & 15)
    hot = jnp.where(
        lax.broadcasted_iota(jnp.int32, (edges, edges), 0) == row, 1.0, 0.0
    ).astype(BF16)
    mirror_msg = dot(hot, got, 0, 0).astype(BF16)
    mirrored = silu(dot(mirror_msg, upr_ref[...])).astype(BF16)
    mixed = ((x_ref[...] + mirrored.astype(F32)) * INV_THREE).astype(BF16)
    for load in loads[0]:
        load.wait()
    inner = silu(dot(mixed, w1[...])).astype(BF16)
    for load in loads[1]:
        load.wait()
    skipped = ((mixed.astype(F32) + silu(dot(inner, w2[...]))) * INV_TWO).astype(BF16)
    skip_ref[...] = skipped
    terms = silu(dot(skipped, proj_ref[...])).astype(BF16)
    atoms = part_ref.shape[0]
    own = jnp.where(
        lax.broadcasted_iota(jnp.int32, (atoms, edges), 0) == src_ref[...], 1.0, 0.0
    ).astype(BF16)
    part_ref[...] = dot(own, terms).astype(BF16)


def atom_kernel(parts_ref, state_ref, w_ref, new_ref, send_ref):
    total = parts_ref[0].astype(F32)
    for i in range(1, NT):
        total = total + parts_ref[i].astype(F32)
    new = (state_ref[...].astype(F32) + silu(dot(total.astype(BF16), w_ref[...]))).astype(BF16)
    new_ref[...] = new
    for i in range(NT):
        send_ref[i] = new


def final_kernel(skip_ref, block_ref, src_ref, back_ref, o_ref):
    atoms = block_ref.shape[0]
    edges = skip_ref.shape[0]
    own = jnp.where(
        lax.broadcasted_iota(jnp.int32, (atoms, edges), 0) == src_ref[...], 1.0, 0.0
    ).astype(BF16)
    feats = dot(own, block_ref[...], 0, 0).astype(BF16)
    o_ref[...] = (skip_ref[...].astype(F32) + silu(dot(feats, back_ref[...]))).astype(BF16)


def shift(d):
    return [(z * YH + h, ((z + d) % Z) * YH + h) for z in range(Z) for h in range(YH)]


def swap():
    return [(i, i ^ 1) for i in range(NS)]


def shift_two():
    return [
        (z * YH + h, ((z + (2 if z % 2 == 0 else -2)) % Z) * YH + h)
        for z in range(Z)
        for h in range(YH)
    ]


def along_x(d):
    return [(t, ((t // 4 + d) % XS) * 4 + t % 4) for t in range(NT)]


def across(bit):
    return [(t, t ^ bit) for t in range(NT)]


def struct(shape, dtype=BF16):
    return jax.ShapeDtypeStruct(shape, dtype)


def local(
    edge_state,
    atom_state,
    edge_source,
    trip_source,
    trip_target,
    trip_count,
    trip_basis,
    reverse_perm,
    down_proj,
    bilinear,
    up_forward,
    up_reverse,
    res_first,
    res_second,
    atom_proj,
    atom_self,
    atom_back,
):
    rows = edge_state[0, 0]
    edges, wide = rows.shape
    width = down_proj.shape[1]
    trips = trip_source.shape[2]

    far = pl.pallas_call(
        down_kernel,
        out_shape=struct((FAR, edges // 2, 2 * width)),
        in_specs=[HB] * 2,
        out_specs=VM,
        scratch_shapes=[
            pltpu.VMEM((edges, wide), BF16),
            pltpu.VMEM((width, wide), BF16),
            pltpu.SemaphoreType.DMA((5,)),
        ],
        compiler_params=params(60),
    )(rows, down_proj.T)

    groups = [[((z0 + 4 * i) % Z) * YH + h for i in range(4)] for z0 in range(4) for h in range(YH)]
    own = lax.all_to_all(
        far, "src", split_axis=0, concat_axis=0, tiled=True, axis_index_groups=groups
    )
    other = lax.ppermute(own, "src", swap())
    own_w = pl.pallas_call(
        pack_kernel,
        out_shape=struct((2,) + res_first.shape),
        in_specs=[HB, VM, VM],
        out_specs=VM,
        compiler_params=params(4),
    )(far, res_first, res_second)
    x_w = [own_w] + [lax.ppermute(own_w, "tgt", along_x(d)) for d in (-1, 2, 1)]
    pieces = []
    for part in (own, other):
        pieces += [part] + [lax.ppermute(part, "src", p) for p in (shift(-1), shift_two(), shift(1))]
    x_w = jnp.stack(x_w)
    y_w = lax.ppermute(x_w, "tgt", across(2))

    my_z = lax.axis_index("src") // YH
    ids = trip_source[0]
    q = ids >> 9
    zq = q >> 1
    other_y = (q ^ lax.axis_index("src")) & 1
    pos = ((other_y * 4 + ((zq - my_z) & 3)) * FAR + (zq >> 2)) * (edges // 2) + (ids & 255)

    tm, send = pl.pallas_call(
        contract_kernel,
        out_shape=(struct((edges, width)), struct((NEAR, Z // 2, 2 * width))),
        in_specs=[SM, SM] + [VM] * 12,
        out_specs=(VM, VM),
        scratch_shapes=[
            pltpu.VMEM((NS * edges // 2, 2 * width), F32),
            pltpu.VMEM((BLOCK, 2 * width), F32),
            pltpu.VMEM((BLOCK, 2 * width), F32),
            pltpu.VMEM((edges, 2 * width), F32),
            pltpu.VMEM((2 * width, edges), F32),
        ],
        compiler_params=params(24),
        cost_estimate=pl.CostEstimate(flops=10**11, bytes_accessed=10**7, transcendentals=0),
    )(
        pos,
        trip_count,
        ids,
        trip_target[0],
        trip_basis[0, 0],
        bilinear.T,
        *pieces,
    )

    plane = [[(z * YH + h) * NT + t for h in range(YH) for t in range(NT)] for z in range(Z)]
    lines = [[z * YH + h for z in range(Z)] for h in range(YH)]
    got = lax.all_to_all(
        send, ("src", "tgt"), split_axis=0, concat_axis=0, tiled=True, axis_index_groups=plane
    )
    turned = pl.pallas_call(
        turn_kernel,
        out_shape=struct((Z, NEAR // 2, 2 * width)),
        in_specs=[VM],
        out_specs=VM,
        scratch_shapes=[pltpu.VMEM((NEAR * Z // 2, 2 * width), F32)],
        compiler_params=params(4),
    )(got)
    turned, x_w, y_w = lax.optimization_barrier((turned, x_w, y_w))
    cx_w = lax.ppermute(x_w, "tgt", across(1))
    cy_w = lax.ppermute(y_w, "tgt", across(1))
    arrived = lax.all_to_all(
        turned, "src", split_axis=0, concat_axis=0, tiled=True, axis_index_groups=lines
    )

    atoms = atom_state.shape[1] * NT
    da = atom_state.shape[2]
    base = pl.pallas_call(
        forward_kernel,
        out_shape=struct((edges, wide), F32),
        in_specs=[VM] * 3,
        out_specs=VM,
        compiler_params=params(12),
        cost_estimate=pl.CostEstimate(flops=10**11, bytes_accessed=10**6, transcendentals=0),
    )(rows, tm, up_forward)
    skipped, part = pl.pallas_call(
        edge_kernel,
        out_shape=(struct((edges, wide)), struct((atoms, da))),
        in_specs=[SM] + [VM] * 6 + [HB] * 4,
        out_specs=(VM, VM),
        scratch_shapes=[
            pltpu.VMEM((wide, wide), BF16),
            pltpu.VMEM((wide, wide), BF16),
            pltpu.SemaphoreType.DMA((2, NT)),
        ],
        compiler_params=params(20),
    )(
        lax.axis_index("tgt").astype(jnp.int32).reshape(1, 1),
        base,
        arrived.reshape(edges // 2, 2 * width),
        reverse_perm[0],
        edge_source[0],
        up_reverse,
        atom_proj,
        x_w,
        y_w,
        cx_w,
        cy_w,
    )

    parts = lax.all_to_all(
        part.reshape(NT, atoms // NT, da), "tgt", split_axis=0, concat_axis=0, tiled=True
    )
    atom_new, spread = pl.pallas_call(
        atom_kernel,
        out_shape=(struct((atoms // NT, da)), struct((NT, atoms // NT, da))),
        in_specs=[VM] * 3,
        out_specs=(VM, VM),
        compiler_params=params(4),
    )(parts, atom_state[0], atom_self)
    block = lax.all_to_all(spread, "tgt", split_axis=0, concat_axis=0, tiled=True)
    edge_new = pl.pallas_call(
        final_kernel,
        out_shape=struct((edges, wide)),
        in_specs=[VM] * 4,
        out_specs=VM,
        compiler_params=params(8),
    )(skipped, block.reshape(atoms, da), edge_source[0], atom_back)
    return (edge_new[None, None], atom_new[None])


def solution(mesh):
    return jax.shard_map(
        local,
        mesh=mesh,
        in_specs=(
            P("src", "tgt", None, None),
            P("src", "tgt", None),
            P("src", "tgt", None),
            P("src", "tgt", None),
            P("src", "tgt", None),
            P("src", "tgt"),
            P("src", "tgt", None, None),
            P("src", "tgt", None),
            P(),
            P(),
            P(),
            P(),
            P("tgt", None),
            P("tgt", None),
            P(),
            P(),
            P(),
        ),
        out_specs=(P("src", "tgt", None, None), P("src", "tgt", None)),
        check_vma=False,
    )
```
